512 devices in a mesh: dp: 32 (over y_lo, z), tensor: 16 (over y_hi, x, core).
Axes of the slice: x: 4, y: 8 (y_hi: 2, y_lo: 4; y = y_hi * 4 + y_lo), z: 8, core: 2. Of those that a mesh axis runs over, the one named last changes fastest.
Arguments:
- features: bfloat16 [65536, 4096], P(('dp', 'tensor')), may hold values from -6 to 6
- step_raw: bfloat16 [65536, 128], P(('dp', 'tensor')), may hold values from -3 to 10
- input_map: bfloat16 [65536, 8, 128], P(('dp', 'tensor')), may hold values from -0.75 to 0.75
- output_map: bfloat16 [65536, 8, 128], P(('dp', 'tensor')), may hold values from -0.75 to 0.75
- decay_log: float32 [128], P('tensor'), may hold values from -10 to -2
- skip_gain: float32 [128], P('tensor'), may hold values from 0.1 to 1.9
- saved_states: bfloat16 [32, 7, 128, 32, 128], P('dp', None, 'tensor'), may hold values from -6 to 6
- grad_out: bfloat16 [65536, 4096], P(('dp', 'tensor')), may hold values from -6 to 6
Outputs:
- grad_features: bfloat16 [65536, 4096], P(('dp', 'tensor'))
- grad_step: float32 [65536, 128], P(('dp', 'tensor'))
- grad_input_map: bfloat16 [65536, 8, 128], P(('dp', 'tensor'))
- grad_output_map: bfloat16 [65536, 8, 128], P(('dp', 'tensor'))
- grad_decay_log: float32 [128], P('tensor')
- grad_skip_gain: float32 [128], P('tensor')
The draws below stay inside these ranges and needn't reach their ends.
All inputs are finite; a program needn't handle non-finite values.
Results may differ from the reference program's by a relative error of at most 0.0013.
Values may be sent and summed in bfloat16 or wider, within the bound.
A program may use at most 128 MiB of HBM per device.

```python
import math
import jax
import jax.numpy as jnp
from jax import lax

SCAN_HEADS = 128
P_SIZE = 32
N = 128
G = 8
Q = 128
SEQUENCE_LENGTH = 2048
NSAVE = 7
REPLICA_ROWS = 65536
N_DP = 32


def draw_step_raw(key, part):
    key = jax.random.fold_in(key, 5)
    first, latter_half, third = jax.random.split(key, 3)
    offset_start = jnp.clip(0.7 * jax.random.normal(first, (REPLICA_ROWS, SCAN_HEADS), jnp.float32) - 0.5, -3.0, 2.0)
    block_group = jax.random.uniform(latter_half, (REPLICA_ROWS, SCAN_HEADS), jnp.float32) < 3.0 / SEQUENCE_LENGTH
    row_extent = jax.random.uniform(third, (REPLICA_ROWS, SCAN_HEADS), jnp.float32, 4.0, 8.0)
    return jnp.where(block_group, offset_start + row_extent, offset_start).astype(jnp.bfloat16)


def draw_decay_log(key, part):
    key = jax.random.fold_in(key, 7)
    lowest = math.log(0.5 / SEQUENCE_LENGTH)
    highest = math.log(0.06)
    values = jax.random.uniform(key, (SCAN_HEADS,), jnp.float32, lowest, highest)
    return values.astype(jnp.float32)


def levels(own_key, shape, cuts, least, largest):
    factor_of = 1.0
    for position, parts in cuts:
        heights = jax.random.uniform(jax.random.fold_in(jax.random.fold_in(own_key, 6), position), (parts,), jnp.float32, least / len(cuts), largest / len(cuts))
        factor_of = factor_of * jnp.repeat(jnp.exp(heights), shape[position] // parts).reshape((-1,) + (1,) * (len(shape) - 1 - position))
    return factor_of


def centred(stream_key, dims, width, bound, cuts=(), held_as=jnp.bfloat16):
    entries = jax.random.normal(stream_key, dims, jnp.float32) * width
    if len(cuts) > 0:
        entries = levels(stream_key, dims, cuts, -0.22, 0.18) * entries
    return jnp.clip(entries, min=-bound, max=bound).astype(held_as)


def setup_inputs(seed: int = 0) -> dict:
    key_list = jax.random.split(jax.random.key(seed), 9)
    features = centred(key_list[0], (REPLICA_ROWS, SCAN_HEADS * P_SIZE), 1.0, 6.0, ((0, 512),))
    step_raw = draw_step_raw(jax.random.fold_in(key_list[8], 71), 0)
    input_map = centred(key_list[2], (REPLICA_ROWS, G, N), 0.125, 0.75, ((0, 512),))
    output_map = centred(key_list[3], (REPLICA_ROWS, G, N), 0.125, 0.75, ((0, 512),))
    decay_log = draw_decay_log(jax.random.fold_in(key_list[8], 71), 0)
    skip_gain = jnp.clip(1.0 + 0.18 * jax.random.normal(key_list[5], (SCAN_HEADS,), jnp.float32), 0.1, 1.9)
    saved_states = centred(key_list[6], (N_DP, NSAVE, SCAN_HEADS, P_SIZE, N), 1.0, 6.0, ((0, 32), (2, 16)))
    grad_out = centred(key_list[7], (REPLICA_ROWS, SCAN_HEADS * P_SIZE), 1.0, 6.0, ((0, 512),))
    return {"features": features, "step_raw": step_raw, "input_map": input_map, "output_map": output_map, "decay_log": decay_log, "skip_gain": skip_gain, "saved_states": saved_states, "grad_out": grad_out}


def head_forward(head_feat, head_raw, head_decay, head_skip, head_in, head_out, head_states):
    block = Q
    stretches = head_feat.shape[0] // block
    pairs = stretches // 2
    exact = lax.Precision.HIGHEST
    step = jax.nn.softplus(head_raw)
    rate = -jnp.exp(head_decay) * step
    cum = jnp.cumsum(rate.reshape(stretches, block), axis=1)
    feat_c = head_feat.reshape(stretches, block, -1)
    in_c = head_in.reshape(stretches, block, -1)
    out_c = head_out.reshape(stretches, block, -1)
    step_c = step.reshape(stretches, block)
    inside = jnp.arange(block)[:, None] >= jnp.arange(block)[None, :]
    spread = cum[:, :, None] - cum[:, None, :]
    decay = jnp.where(inside, jnp.exp(jnp.where(inside, spread, 0.0)), 0.0)
    scores = jnp.einsum('cin,cjn->cij', out_c, in_c, precision=exact) * decay * step_c[:, None, :]
    within = jnp.einsum('cij,cjp->cip', scores, feat_c, precision=exact)
    weight_end = jnp.exp(cum[:, -1:] - cum) * step_c
    added = jnp.einsum('cjp,cjn->cpn', feat_c * weight_end[:, :, None], in_c, precision=exact)
    falloff = jnp.exp(cum[:, -1])
    saved_pad = jnp.concatenate([head_states, jnp.zeros_like(head_states[:1])], axis=0)
    following = jnp.stack([jnp.zeros_like(saved_pad), saved_pad], axis=1).reshape(stretches, head_states.shape[1], head_states.shape[2])
    resets = jnp.tile(jnp.array([0.0, 1.0], jnp.float32), pairs)

    def advance(state, items):
        factor, extra, coming, reset = items
        made = factor * state + extra
        return (made + reset * (coming - lax.stop_gradient(made)), state)
    start_state = jnp.zeros((head_states.shape[1], head_states.shape[2]), jnp.float32)
    ending, entering = lax.scan(advance, start_state, (falloff, added, following, resets))
    across = jnp.einsum('cin,cpn->cip', out_c * jnp.exp(cum)[:, :, None], entering, precision=exact)
    return (within + across).reshape(head_feat.shape) + head_skip * head_feat

def reference(features, step_raw, input_map, output_map, decay_log, skip_gain, saved_states, grad_out):
    per_group = SCAN_HEADS // G

    def replica(index):
        start = index * SEQUENCE_LENGTH
        feats = lax.dynamic_slice_in_dim(features, start, SEQUENCE_LENGTH, 0).astype(jnp.float32).reshape(SEQUENCE_LENGTH, SCAN_HEADS, P_SIZE)
        cotan = lax.dynamic_slice_in_dim(grad_out, start, SEQUENCE_LENGTH, 0).astype(jnp.float32).reshape(SEQUENCE_LENGTH, SCAN_HEADS, P_SIZE)
        raws = lax.dynamic_slice_in_dim(step_raw, start, SEQUENCE_LENGTH, 0).astype(jnp.float32)
        inputs = lax.dynamic_slice_in_dim(input_map, start, SEQUENCE_LENGTH, 0).astype(jnp.float32)
        outputs = lax.dynamic_slice_in_dim(output_map, start, SEQUENCE_LENGTH, 0).astype(jnp.float32)
        states = lax.dynamic_index_in_dim(saved_states, index, 0, keepdims=False).astype(jnp.float32)

        def one_head(head):
            group = head // per_group
            head_feat = lax.dynamic_index_in_dim(feats, head, 1, keepdims=False)
            head_cot = lax.dynamic_index_in_dim(cotan, head, 1, keepdims=False)
            head_raw = lax.dynamic_index_in_dim(raws, head, 1, keepdims=False)
            head_in = lax.dynamic_index_in_dim(inputs, group, 1, keepdims=False)
            head_out = lax.dynamic_index_in_dim(outputs, group, 1, keepdims=False)
            head_decay = lax.dynamic_index_in_dim(decay_log, head, 0, keepdims=False)
            head_skip = lax.dynamic_index_in_dim(skip_gain, head, 0, keepdims=False)
            head_states = lax.dynamic_index_in_dim(states, head, 1, keepdims=False)

            def forward(a_feat, a_raw, a_decay, a_skip, a_in, a_out):
                return head_forward(a_feat, a_raw, a_decay, a_skip, a_in, a_out, head_states)
            ignored, pull = jax.vjp(forward, head_feat, head_raw, head_decay, head_skip, head_in, head_out)
            return pull(head_cot)
        pieces = lax.map(one_head, jnp.arange(SCAN_HEADS, dtype=jnp.int32))
        grad_feat = jnp.transpose(pieces[0], (1, 0, 2)).reshape(SEQUENCE_LENGTH, SCAN_HEADS * P_SIZE).astype(jnp.bfloat16)
        grad_raw = jnp.transpose(pieces[1])
        grad_in = jnp.transpose(pieces[4].reshape(G, per_group, SEQUENCE_LENGTH, N).sum(axis=1), (1, 0, 2)).astype(jnp.bfloat16)
        grad_outmap = jnp.transpose(pieces[5].reshape(G, per_group, SEQUENCE_LENGTH, N).sum(axis=1), (1, 0, 2)).astype(jnp.bfloat16)
        return (grad_feat, grad_raw, grad_in, grad_outmap, pieces[2], pieces[3])
    results = lax.map(replica, jnp.arange(N_DP, dtype=jnp.int32))
    return (results[0].reshape(REPLICA_ROWS, SCAN_HEADS * P_SIZE), results[1].reshape(REPLICA_ROWS, SCAN_HEADS), results[2].reshape(REPLICA_ROWS, G, N), results[3].reshape(REPLICA_ROWS, G, N), lax.optimization_barrier(jnp.sum(results[4], axis=0)), lax.optimization_barrier(jnp.sum(results[5], axis=0)))
```

```python
import functools

import jax
import jax.numpy as jnp
from jax import lax
from jax.experimental import pallas as pl
from jax.experimental.pallas import tpu as pltpu
from jax.sharding import PartitionSpec as P

MESH = pl.DeviceIdType.MESH
F32 = jnp.float32
BF16 = jnp.bfloat16
VMEM = pltpu.VMEM
LIMIT = 56 * 1024 * 1024

Q = 128
N = 128
PW = 32
HEADS = 128
GROUPS = 8
PER = HEADS // GROUPS
ROWS = PER * PW


def split2(x):
    hi = x.astype(BF16)
    return hi, (x - hi.astype(F32)).astype(BF16)


def split3(x):
    hi = x.astype(BF16)
    rest = x - hi.astype(F32)
    mid = rest.astype(BF16)
    return hi, mid, (rest - mid.astype(F32)).astype(BF16)


def mm(a, b, ca=1, cb=0):
    return lax.dot_general(a, b, (((ca,), (cb,)), ((), ())), preferred_element_type=F32)


def lane_sums(x, ones):
    return mm(jnp.concatenate(split3(x), axis=1), jnp.concatenate([ones] * 3, axis=0))


def iota(dim):
    return lax.broadcasted_iota(jnp.int32, (Q, Q), dim)


def expand(x):
    return jnp.broadcast_to(x[:, None, :], (x.shape[0], PW, x.shape[1])).reshape(-1, x.shape[1])


def head_sums(x):
    return x.reshape(-1, PW, x.shape[1]).sum(axis=1)


def peer_barrier(me, count):
    barrier = pltpu.get_barrier_semaphore()

    def greet(j, carry):
        peer = lax.rem(me + j, count)
        pl.semaphore_signal(barrier, inc=1, device_id={"tensor": peer}, device_id_type=MESH)
        return carry

    lax.fori_loop(1, count, greet, 0)
    pl.semaphore_wait(barrier, count - 1)


def prep_kernel(
    raw_ref, own_ref, x_ref, y_ref, b_ref, c_ref,
    cum_ref, v_ref, s_ref, sig_ref, a_ref, skip_ref, f_ref, xt_ref, yt_ref, d_ref, add_ref,
    gath, e_scr, w_scr, send_sem, recv_sem,
):
    me = lax.axis_index("tensor")
    count = gath.shape[0]
    peer_barrier(me, count)

    def copy_to(j):
        return pltpu.make_async_remote_copy(
            src_ref=own_ref, dst_ref=gath.at[me], send_sem=send_sem.at[j], recv_sem=recv_sem.at[j],
            device_id={"tensor": lax.rem(me + j, count)}, device_id_type=MESH,
        )

    def start(j, carry):
        copy_to(j).start()
        return carry

    def finish(j, carry):
        copy_to(j).wait()
        return carry

    lax.fori_loop(1, count, start, 0)
    gath[me] = own_ref[...]

    raw = raw_ref[...].astype(F32).T
    small = jnp.exp(-jnp.abs(raw))
    s = jnp.maximum(raw, 0.0) + jnp.log1p(small)
    sig_ref[...] = jnp.where(raw >= 0, 1.0, small) / (1.0 + small)
    s_ref[...] = s

    lax.fori_loop(1, count, finish, 0)
    a = jnp.exp(gath[:, 0:8, :].reshape(HEADS, Q))
    skip_ref[...] = gath[:, 8:16, :].reshape(HEADS, Q)
    a_ref[...] = a
    cum = lane_sums(-a * s, (iota(0) <= iota(1)).astype(F32).astype(BF16))
    last = jnp.broadcast_to(cum[:, Q - 1 : Q], (HEADS, Q))
    cum_ref[...] = cum
    v_ref[...] = cum - jnp.log(s)
    f_ref[...] = jnp.exp(last)
    e_scr[...] = jnp.exp(cum)
    w_scr[...] = jnp.exp(last - cum) * s

    def group(g, carry):
        lanes = pl.ds(pl.multiple_of(g * ROWS, ROWS), ROWS)
        heads = pl.ds(pl.multiple_of(g * PER, PER), PER)
        maps = pl.ds(pl.multiple_of(g * N, N), N)
        for src, dst, scale, m_ref, out in (
            (y_ref, yt_ref, e_scr, c_ref, d_ref),
            (x_ref, xt_ref, w_scr, b_ref, add_ref),
        ):
            turned = src[:, lanes].astype(F32).T
            dst[lanes, :] = turned.astype(BF16)
            hi, lo = split2(turned * expand(scale[heads, :]))
            m = m_ref[:, maps]
            out[lanes, :] = mm(jnp.concatenate([hi, lo], axis=1), jnp.concatenate([m, m], axis=0))
        return carry

    lax.fori_loop(0, GROUPS, group, 0)


def chain_kernel(
    d_ref, f_ref, add_ref, saved_ref,
    g_ref, e_ref,
    dsib, fsib, chain_in, chain_out, gsib_out, gsib_in, esaved, made_out, made_in,
    sems_s, sems_r,
):
    me = lax.axis_index("tensor")
    count = esaved.shape[0]
    core = lax.rem(me, 2)
    pair = me // 2
    pairs = count // 2
    sib = me + 1 - 2 * core
    half = count // 2
    peer_barrier(me, count)

    def rcopy(src, dst, s_sem, r_sem, dev):
        return pltpu.make_async_remote_copy(
            src_ref=src, dst_ref=dst, send_sem=s_sem, recv_sem=r_sem, device_id={"tensor": dev}, device_id_type=MESH
        )

    def d_copy(u):
        return rcopy(
            d_ref.at[(1 - core) * half + u], dsib.at[u], sems_s.at[u], sems_r.at[u], sib
        )

    def chain_copy(u):
        return rcopy(chain_out.at[u], chain_in.at[u], sems_s.at[16 + u], sems_r.at[16 + u], me - 2)

    def g_copy(u):
        return rcopy(gsib_out.at[u], gsib_in.at[u], sems_s.at[32 + u], sems_r.at[32 + u], sib)

    def saved_send(k):
        return rcopy(saved_ref.at[k - 1], esaved.at[me], sems_s.at[48 + k], sems_r.at[48 + me], 2 * k)

    def saved_recv(t):
        return rcopy(saved_ref.at[0], esaved.at[t], sems_s.at[48], sems_r.at[48 + t], sib)

    def made_copy(t):
        return rcopy(made_out.at[t], made_in.at[t], sems_s.at[64 + t], sems_r.at[64 + t], sib)

    f_copy = rcopy(f_ref, fsib, sems_s.at[80], sems_r.at[80], sib)

    def loop(lo, hi, body):
        def step(i, carry):
            body(i)
            return carry

        lax.fori_loop(lo, hi, step, 0)

    f_copy.start()
    loop(0, half, lambda u: d_copy(u).start())

    def send_saved(k):
        @pl.when(me != 2 * k)
        def _():
            saved_send(k).start()

        @pl.when(me == 2 * k)
        def _():
            esaved[me] = saved_ref[k - 1]

    loop(1, pairs, send_saved)

    f_copy.wait_recv()

    def chain_step(u):
        q = core * half + u
        heads = pl.ds(pl.multiple_of(q * 8, 8), 8)
        f_own, f_sib = f_ref[heads, :], fsib[heads, :]
        d_copy(u).wait_recv()
        d_own, d_sib = d_ref[q], dsib[u]
        even = core == 0
        d_even, d_odd = jnp.where(even, d_own, d_sib), jnp.where(even, d_sib, d_own)
        f_even, f_odd = jnp.where(even, f_own, f_sib), jnp.where(even, f_sib, f_own)
        f_odd = expand(f_odd)
        f_even = expand(f_even)

        @pl.when(pair < pairs - 1)
        def _():
            chain_copy(u).wait_recv()

        @pl.when(pair == pairs - 1)
        def _():
            chain_in[u] = jnp.zeros_like(d_own)

        coming = chain_in[u]
        to_even = d_odd + f_odd * coming

        @pl.when(pair > 0)
        def _():
            chain_out[u] = d_even + f_even * to_even
            chain_copy(u).start()

        g_ref[q] = jnp.where(even, to_even, coming)
        gsib_out[u] = jnp.where(even, coming, to_even)
        g_copy(u).start()

    loop(0, half, chain_step)

    def even_states(t):
        @pl.when(pair > 0)
        def _():
            @pl.when(t != me)
            def _():
                saved_recv(t).wait_recv()

            e_ref[t] = esaved[t].astype(F32)

        @pl.when(pair == 0)
        def _():
            e_ref[t] = jnp.zeros(e_ref.shape[1:], F32)

        heads = pl.ds(pl.multiple_of(t * 8, 8), 8)
        made_out[t] = expand(f_ref[heads, :]) * e_ref[t] + add_ref[t]
        made_copy(t).start()

    def odd_states(t):
        made_copy(t).wait_recv()
        e_ref[t] = made_in[t]

    @pl.when(core == 0)
    def _():
        loop(0, count, even_states)
        loop(0, count, lambda t: made_copy(t).wait_send())

    @pl.when(core == 1)
    def _():
        loop(0, count, odd_states)

    def sib_g(u):
        g_copy(u).wait()
        g_ref[(1 - core) * half + u] = gsib_in[u]
        d_copy(u).wait_send()

        @pl.when(pair > 0)
        def _():
            chain_copy(u).wait_send()

    loop(0, half, sib_g)
    f_copy.wait_send()

    def saved_sent(k):
        @pl.when(me != 2 * k)
        def _():
            saved_send(k).wait_send()

    loop(1, pairs, saved_sent)


def main_kernel(
    xt_ref, yt_ref, y_ref, b_ref, c_ref, cum_ref, v_ref, s_ref, sig_ref, a_ref, skip_ref, f_ref, e_ref, g_ref,
    dx_ref, draw_ref, db_ref, dc_ref, z_ref,
    dxt, u_scr, r_scr, draw_scr,
):
    g = pl.program_id(0)
    b, c = b_ref[...], c_ref[...]
    m = mm(c, b, 1, 1)
    cum, v, s = cum_ref[...], v_ref[...], s_ref[...]
    cum_n = cum.T
    inside = iota(0) >= iota(1)
    head_of = iota(0) // PW
    dm = jnp.zeros((Q, Q), F32)
    for q in range(PER // 4):
        rows = slice(q * Q, (q + 1) * Q)
        x4 = xt_ref[rows, :]
        wide = jnp.concatenate([jnp.where(head_of == h, x4.astype(F32), 0.0).astype(BF16) for h in range(4)], axis=1)
        ds4 = mm(y_ref[:, rows], wide)
        for h in range(4):
            hh = 4 * q + h
            mine = slice(q * Q + h * PW, q * Q + (h + 1) * PW)
            xh, yh = xt_ref[mine, :], yt_ref[mine, :]
            spread = cum_n[:, hh : hh + 1] - v[hh : hh + 1, :]
            decay = jnp.exp(jnp.where(inside, spread, -1e30))
            scores = m * decay
            dm = dm + ds4[:, h * Q : (h + 1) * Q] * decay
            both = jnp.concatenate(split2(scores), axis=0)
            dxw = mm(jnp.concatenate([yh, yh], axis=1), both)
            within = mm(xh, both, 1, 1)
            within = within[:, :Q] + within[:, Q:]
            dxt[mine, :] = dxw
            u_scr[hh : hh + 1, :] = jnp.sum(xh.astype(F32) * dxw, axis=0, keepdims=True)
            r_scr[hh : hh + 1, :] = jnp.sum(yh.astype(F32) * within, axis=0, keepdims=True)

    xt, yt = xt_ref[...].astype(F32), yt_ref[...].astype(F32)
    e_state, g_state = e_ref[...], g_ref[...]
    e_hi, e_lo = split2(e_state)
    g_hi, g_lo = split2(g_state)
    last = jnp.broadcast_to(cum[:, Q - 1 : Q], cum.shape)
    w = jnp.exp(last - cum) * s
    ex_w = expand(w)
    ey = expand(jnp.exp(cum)) * yt
    wx = ex_w * xt
    ec = mm(jnp.concatenate([e_hi, e_lo], axis=1), jnp.concatenate([c, c], axis=1), 1, 1)
    gb = mm(jnp.concatenate([g_hi, g_lo], axis=1), jnp.concatenate([b, b], axis=1), 1, 1)
    across = head_sums(ey * ec)
    ends = head_sums(wx * gb)

    dm_hi, dm_lo = split2(dm)
    ey_hi, ey_lo = split2(ey)
    wx_hi, wx_lo = split2(wx)
    dc = mm(jnp.concatenate([dm_hi, dm_lo], axis=1), jnp.concatenate([b, b], axis=0))
    dc = dc + mm(ey_hi, e_hi, 0, 0) + mm(ey_hi, e_lo, 0, 0) + mm(ey_lo, e_hi, 0, 0)
    dc_ref[...] = dc.astype(BF16)
    db = mm(jnp.concatenate([dm_hi, dm_lo], axis=0), jnp.concatenate([c, c], axis=0), 0, 0)
    db = db + mm(wx_hi, g_hi, 0, 0) + mm(wx_hi, g_lo, 0, 0) + mm(wx_lo, g_hi, 0, 0)
    db_ref[...] = db.astype(BF16)

    dx = dxt[...] + ex_w * gb + expand(skip_ref[...]) * yt
    dx_ref[...] = dx.T.astype(BF16)

    a, u, r = a_ref[...], u_scr[...], r_scr[...]
    through = jnp.sum(head_sums(e_state * g_state), axis=1, keepdims=True) * f_ref[...]
    at_end = through + jnp.sum(ends, axis=1, keepdims=True)
    lane = lax.broadcasted_iota(jnp.int32, (PER, Q), 1)
    dcum = r - u + across - ends + jnp.where(lane == Q - 1, at_end, 0.0)
    drate = lane_sums(dcum, (iota(0) >= iota(1)).astype(F32).astype(BF16))
    draw_scr[pl.ds(pl.multiple_of(g * PER, PER), PER), :] = (-a * drate + (u + ends) / s) * sig_ref[...]
    decay_part = jnp.sum(drate * (-a * s), axis=1, keepdims=True)
    skip_part = jnp.sum(head_sums(yt * xt), axis=1, keepdims=True)
    z_ref[...] = jnp.where(lane < Q // 2, decay_part, skip_part)

    @pl.when(g == GROUPS - 1)
    def _():
        draw_ref[...] = draw_scr[...].T


def total_kernel(dp_inner, z_ref, out_ref, part, from_t, from_i, from_o, send_sem, recv_sem):
    me = lax.axis_index("tensor")
    row = lax.axis_index("dp")
    n_t = from_t.shape[0]
    n_i, n_o = from_i.shape[0], from_o.shape[0]
    inner, outer = lax.rem(row, dp_inner), row // dp_inner

    def loop(lo, hi, body):
        def step(i, carry):
            body(i)
            return carry

        lax.fori_loop(lo, hi, step, 0)

    def dev_t(j):
        return {"tensor": lax.rem(me + j, n_t)}

    def dev_i(j):
        return {"dp": outer * dp_inner + lax.rem(inner + j, n_i)}

    def dev_o(j):
        return {"dp": lax.rem(outer + j, n_o) * dp_inner + inner}

    barrier = pltpu.get_barrier_semaphore()
    for n, dev in ((n_t, dev_t), (n_i, dev_i), (n_o, dev_o)):
        loop(1, n, lambda j: pl.semaphore_signal(barrier, inc=1, device_id=dev(j), device_id_type=MESH))
    pl.semaphore_wait(barrier, n_t - 1 + n_i - 1 + n_o - 1)

    def exchange(n, dev, at, source, landing, base):
        def copy(j):
            return pltpu.make_async_remote_copy(
                src_ref=source(j), dst_ref=landing.at[at],
                send_sem=send_sem.at[base + j], recv_sem=recv_sem.at[base + j],
                device_id=dev(j), device_id_type=MESH,
            )

        loop(1, n, lambda j: copy(j).start())
        landing[at] = source(0)[...]
        loop(1, n, lambda j: copy(j).wait())
        return jnp.sum(landing[...], axis=0)

    part[0] = exchange(n_t, dev_t, me, lambda j: z_ref.at[lax.rem(me + j, n_t)], from_t, 0)
    part[1] = exchange(n_i, dev_i, inner, lambda j: part.at[0], from_i, n_t)
    out_ref[...] = exchange(n_o, dev_o, outer, lambda j: part.at[1], from_o, n_t + n_i)


def on_device(features, step_raw, input_map, output_map, decay_log, skip_gain, saved_states, grad_out):
    n_t = lax.axis_size("tensor")
    n_dp = lax.axis_size("dp")
    b = input_map.reshape(Q, GROUPS * N)
    c = output_map.reshape(Q, GROUPS * N)
    own = jnp.broadcast_to(jnp.concatenate([decay_log, skip_gain])[:, None], (16, Q))
    table = jax.ShapeDtypeStruct((HEADS, Q), F32)
    turned = jax.ShapeDtypeStruct((HEADS * PW, Q), BF16)
    states = jax.ShapeDtypeStruct((HEADS * PW, N), F32)
    whole = pl.BlockSpec(memory_space=VMEM)

    def params(cid=None):
        if cid is None:
            return pltpu.CompilerParams(vmem_limit_bytes=LIMIT)
        return pltpu.CompilerParams(vmem_limit_bytes=LIMIT, collective_id=cid, has_side_effects=True)

    cum, v, s, sig, a, skip, f, xt, yt, d, add = pl.pallas_call(
        prep_kernel,
        out_shape=[table] * 7 + [turned] * 2 + [states] * 2,
        in_specs=[whole] * 6,
        out_specs=[whole] * 11,
        scratch_shapes=[
            VMEM((n_t, 16, Q), F32), VMEM((HEADS, Q), F32), VMEM((HEADS, Q), F32),
            pltpu.SemaphoreType.DMA((n_t,)), pltpu.SemaphoreType.DMA((n_t,)),
        ],
        compiler_params=params(0),
        name="prep",
    )(step_raw, own, features, grad_out, b, c)

    chunk = HEADS * PW // n_t
    half = n_t // 2
    chunks = jax.ShapeDtypeStruct((n_t, chunk, N), F32)
    halves = VMEM((half, chunk, N), F32)
    g_state, e_state = pl.pallas_call(
        chain_kernel,
        out_shape=[chunks, chunks],
        in_specs=[whole] * 4,
        out_specs=[whole] * 2,
        scratch_shapes=[
            halves, VMEM((HEADS, Q), F32), halves, halves, halves, halves,
            VMEM((n_t, chunk, N), BF16), VMEM((n_t, chunk, N), F32), VMEM((n_t, chunk, N), F32),
            pltpu.SemaphoreType.DMA((81,)), pltpu.SemaphoreType.DMA((81,)),
        ],
        compiler_params=params(1),
        name="chain",
    )(d.reshape(chunks.shape), f, add.reshape(chunks.shape), saved_states.reshape(-1, chunk, N))

    by_head = pl.BlockSpec((PER, Q), lambda g: (g, 0))
    by_row = pl.BlockSpec((ROWS, Q), lambda g: (g, 0))
    by_map = pl.BlockSpec((Q, N), lambda g: (0, g))
    by_lane = pl.BlockSpec((Q, ROWS), lambda g: (0, g))
    dx, draw, db, dc, z = pl.pallas_call(
        main_kernel,
        grid=(GROUPS,),
        out_shape=[
            jax.ShapeDtypeStruct((Q, HEADS * PW), BF16),
            jax.ShapeDtypeStruct((Q, HEADS), F32),
            jax.ShapeDtypeStruct((Q, GROUPS * N), BF16),
            jax.ShapeDtypeStruct((Q, GROUPS * N), BF16),
            table,
        ],
        in_specs=[by_row, by_row, by_lane, by_map, by_map] + [by_head] * 7 + [by_row] * 2,
        out_specs=[by_lane, pl.BlockSpec((Q, HEADS), lambda g: (0, 0)), by_map, by_map, by_head],
        scratch_shapes=[VMEM((ROWS, Q), F32), VMEM((PER, Q), F32), VMEM((PER, Q), F32), VMEM((HEADS, Q), F32)],
        compiler_params=params(),
        name="main",
    )(xt, yt, grad_out, b, c, cum, v, s, sig, a, skip, f, e_state.reshape(states.shape), g_state.reshape(states.shape))

    dp_inner = 8 if n_dp % 8 == 0 else n_dp
    dp_outer = n_dp // dp_inner
    sums = n_t + dp_inner + dp_outer
    total = pl.pallas_call(
        functools.partial(total_kernel, dp_inner),
        out_shape=jax.ShapeDtypeStruct((8, Q), F32),
        in_specs=[whole],
        out_specs=whole,
        scratch_shapes=[
            VMEM((2, 8, Q), F32),
            VMEM((n_t, 8, Q), F32), VMEM((dp_inner, 8, Q), F32), VMEM((dp_outer, 8, Q), F32),
            pltpu.SemaphoreType.DMA((sums,)), pltpu.SemaphoreType.DMA((sums,)),
        ],
        compiler_params=params(2),
        name="total",
    )(z.reshape(n_t, 8, Q))
    return (
        dx,
        draw,
        db.reshape(Q, GROUPS, N),
        dc.reshape(Q, GROUPS, N),
        total[:, 0],
        total[:, Q // 2],
    )


def solution(mesh):
    placed = (
        P(("dp", "tensor"), None),
        P(("dp", "tensor"), None),
        P(("dp", "tensor"), None, None),
        P(("dp", "tensor"), None, None),
        P("tensor"),
        P("tensor"),
        P("dp", None, "tensor", None, None),
        P(("dp", "tensor"), None),
    )
    return jax.shard_map(
        on_device,
        mesh=mesh,
        in_specs=placed,
        out_specs=(
            P(("dp", "tensor"), None),
            P(("dp", "tensor"), None),
            P(("dp", "tensor"), None, None),
            P(("dp", "tensor"), None, None),
            P("tensor"),
            P("tensor"),
        ),
        check_vma=False,
    )
```

```python
import functools

import jax
import jax.numpy as jnp
from jax import lax
from jax.experimental import pallas as pl
from jax.experimental.pallas import tpu as pltpu
from jax.sharding import PartitionSpec as P

MESH = pl.DeviceIdType.MESH
F32 = jnp.float32
BF16 = jnp.bfloat16
VMEM = pltpu.VMEM
LIMIT = 56 * 1024 * 1024

Q = 128
N = 128
PW = 32
HEADS = 128
GROUPS = 8
PER = HEADS // GROUPS
ROWS = PER * PW


def split2(x):
    hi = x.astype(BF16)
    return hi, (x - hi.astype(F32)).astype(BF16)


def split3(x):
    hi = x.astype(BF16)
    rest = x - hi.astype(F32)
    mid = rest.astype(BF16)
    return hi, mid, (rest - mid.astype(F32)).astype(BF16)


def mm(a, b, ca=1, cb=0):
    return lax.dot_general(a, b, (((ca,), (cb,)), ((), ())), preferred_element_type=F32)


def lane_sums(x, ones):
    return mm(jnp.concatenate(split3(x), axis=1), jnp.concatenate([ones] * 3, axis=0))


def iota(dim):
    return lax.broadcasted_iota(jnp.int32, (Q, Q), dim)


def expand(x):
    return jnp.broadcast_to(x[:, None, :], (x.shape[0], PW, x.shape[1])).reshape(-1, x.shape[1])


def head_sums(x):
    return x.reshape(-1, PW, x.shape[1]).sum(axis=1)

CHIPS = 4
SUBS = 4
SUB = ROWS // SUBS
HEADS_SUB = PER // SUBS
WIRE = SUB + 8


def loop(lo, hi, body):
    def step(i, carry):
        body(i)
        return carry

    lax.fori_loop(lo, hi, step, 0)


def spans(i, size):
    return pl.ds(pl.multiple_of(i * size, size), size)


def kernel(
    dp_inner,
    raw_ref, own_ref, x_ref, y_ref, b_ref, c_ref, saved_ref,
    dx_ref, draw_ref, db_ref, dc_ref, total_ref,
    gath, cum_s, v_s, s_s, sig_s, a_s, skip_s, f_s, e_s, w_s, fsib, u_s, r_s, drate_s, z_s,
    bm, cm, wide_f32, xt, yt, d_s, dsib, comp, cin, rout, yout, yin, rin, gst, gout,
    esaved, est, mout, dxt, db_acc, dc_acc,
    part, from_t, from_i, from_o,
    own_sem, saved_sem, f_sem, d_sem, in_sem, y_sem, ret_sem, g_sem, made_sem, sum_sem,
):
    me = lax.axis_index("tensor")
    rep = lax.axis_index("dp")
    n_t, n_i, n_o = from_t.shape[0], from_i.shape[0], from_o.shape[0]
    core = lax.rem(me, 2)
    even = core == 0
    pair = me // 2
    x = lax.rem(pair, CHIPS)
    row = pair // CHIPS
    sib = me + 1 - 2 * core
    inner, outer = lax.rem(rep, dp_inner), rep // dp_inner
    last_pair = pair == n_t // 2 - 1

    def dev_t(j):
        return {"tensor": lax.rem(me + j, n_t)}

    def dev_i(j):
        return {"dp": outer * dp_inner + lax.rem(inner + j, n_i)}

    def dev_o(j):
        return {"dp": lax.rem(outer + j, n_o) * dp_inner + inner}

    def remote(src, dst, sems, i, j, dev):
        return pltpu.make_async_remote_copy(
            src_ref=src, dst_ref=dst, send_sem=sems.at[(0, *i)], recv_sem=sems.at[(1, *j)],
            device_id=dev, device_id_type=MESH,
        )

    barrier = pltpu.get_barrier_semaphore()
    for n, dev in ((n_t, dev_t), (n_i, dev_i), (n_o, dev_o)):
        loop(1, n, lambda j: pl.semaphore_signal(barrier, inc=1, device_id=dev(j), device_id_type=MESH))
    pl.semaphore_wait(barrier, n_t - 1 + n_i - 1 + n_o - 1)

    def own_copy(j):
        return remote(own_ref, gath.at[me], own_sem, (j,), (j,), dev_t(j))

    def saved_copy(k):
        return remote(saved_ref.at[k - 1], esaved.at[me], saved_sem, (k,), (me,), {"tensor": 2 * k})

    def saved_arrival(t):
        return remote(saved_ref.at[0], esaved.at[t], saved_sem, (0,), (t,), {"tensor": sib})

    def send_saved(k):
        @pl.when(me != 2 * k)
        def _():
            saved_copy(k).start()

        @pl.when(me == 2 * k)
        def _():
            esaved[me] = saved_ref[k - 1]

    loop(1, n_t, lambda j: own_copy(j).start())
    loop(1, n_t // 2, send_saved)
    gath[me] = own_ref[...]

    raw = raw_ref[...].astype(F32).T
    small = jnp.exp(-jnp.abs(raw))
    s = jnp.maximum(raw, 0.0) + jnp.log1p(small)
    sig_s[...] = (jnp.where(raw >= 0, 1.0, small) / (1.0 + small)).reshape(sig_s.shape)
    s_s[...] = s.reshape(s_s.shape)
    for src, dst in ((b_ref, bm), (c_ref, cm)):
        wide_f32[...] = src[...].astype(F32)
        for g in range(GROUPS):
            dst[g] = wide_f32[pl.ds(g, Q, stride=GROUPS), :].astype(BF16)

    def turn(g):
        for src, dst in ((y_ref, yt), (x_ref, xt)):
            dst[g] = src[:, spans(g, ROWS)].astype(F32).T.astype(BF16)

    loop(0, GROUPS, turn)

    loop(1, n_t, lambda j: own_copy(j).wait())
    a = jnp.exp(gath[:, 0:8, :].reshape(HEADS, Q))
    skip_s[...] = gath[:, 8:16, :].reshape(skip_s.shape)
    a_s[...] = a.reshape(a_s.shape)
    cum = lane_sums(-a * s, (iota(0) <= iota(1)).astype(F32).astype(BF16))
    last = jnp.broadcast_to(cum[:, Q - 1 : Q], (HEADS, Q))
    cum_s[...] = cum.reshape(cum_s.shape)
    v_s[...] = (cum - jnp.log(s)).reshape(v_s.shape)
    f_s[...] = jnp.exp(last).reshape(f_s.shape)
    e_s[...] = jnp.exp(cum).reshape(e_s.shape)
    w_s[...] = (jnp.exp(last - cum) * s).reshape(w_s.shape)
    f_copy = remote(f_s, fsib, f_sem, (0,), (0,), {"tensor": sib})
    f_copy.start()

    def d_copy(q):
        return remote(d_s.at[2 * q + 1 - core], dsib.at[q], d_sem, (q,), (q,), {"tensor": sib})

    def made_of(g):
        hi, lo = split2(yt[g].astype(F32) * expand(e_s[g]))
        m = cm[g]
        both = mm(jnp.concatenate([hi, lo], axis=1), jnp.concatenate([m, m], axis=0))
        d_s[g] = both.reshape(SUBS, SUB, N)

    def first_half(q):
        made_of(2 * q + 1 - core)
        d_copy(q).start()

    loop(0, CHIPS, first_half)
    loop(0, CHIPS, lambda q: made_of(2 * q + core))

    def in_copy(q, t):
        return remote(
            comp.at[q, t], cin.at[x, t], in_sem, (q, t), (x, t), {"tensor": row * 2 * CHIPS + 2 * q + core}
        )

    def in_arrival(j, t):
        return remote(comp.at[j, t], cin.at[j, t], in_sem, (j, t), (j, t), {"tensor": sib})

    f_copy.wait()

    def fold(q):
        g = 2 * q + core
        f_own, f_sib = f_s[g], fsib[g]
        f_even, f_odd = jnp.where(even, f_own, f_sib), jnp.where(even, f_sib, f_own)
        d_copy(q).wait_recv()
        for t in range(SUBS):
            hs = slice(t * HEADS_SUB, (t + 1) * HEADS_SUB)
            d_own, d_sib = d_s[g, t], dsib[q, t]
            d_even, d_odd = jnp.where(even, d_own, d_sib), jnp.where(even, d_sib, d_own)
            comp[q, t, 0:SUB, :] = d_even + expand(f_even[hs]) * d_odd
            f_both = (f_even * f_odd)[hs]
            comp[q, t, SUB:WIRE, :] = jnp.concatenate([f_both, f_both], axis=0)

        @pl.when(q != x)
        def _():
            for t in range(SUBS):
                in_copy(q, t).start()

        @pl.when(q == x)
        def _():
            cin[x] = comp[q]

    loop(0, CHIPS, fold)

    inside = iota(0) >= iota(1)
    head_of = iota(0) // PW

    def local(g):
        b, c = bm[g], cm[g]
        m = mm(c, b, 1, 1)
        v = v_s[g]
        cum_n = cum_s[g].T
        dm = jnp.zeros((Q, Q), F32)
        for q in range(PER // 4):
            x4 = xt[g, q * Q : (q + 1) * Q, :].astype(F32)
            wide = jnp.concatenate([jnp.where(head_of == h, x4, 0.0).astype(BF16) for h in range(4)], axis=1)
            y4 = y_ref[:, pl.ds(pl.multiple_of(g * ROWS + q * Q, Q), Q)]
            ds4 = mm(y4, wide)
            for h in range(4):
                hh = 4 * q + h
                mine = slice(hh * PW, (hh + 1) * PW)
                xh, yh = xt[g, mine, :], yt[g, mine, :]
                spread = cum_n[:, hh : hh + 1] - v[hh : hh + 1, :]
                decay = jnp.exp(jnp.where(inside, spread, -1e30))
                scores = m * decay
                dm = dm + ds4[:, h * Q : (h + 1) * Q] * decay
                both = jnp.concatenate(split2(scores), axis=0)
                dxw = mm(jnp.concatenate([yh, yh], axis=1), both)
                within = mm(xh, both, 1, 1)
                within = within[:, :Q] + within[:, Q:]
                dxt[g, mine, :] = dxw
                u_s[g, hh : hh + 1, :] = jnp.sum(xh.astype(F32) * dxw, axis=0, keepdims=True)
                r_s[g, hh : hh + 1, :] = jnp.sum(yh.astype(F32) * within, axis=0, keepdims=True)
        dm_hi, dm_lo = split2(dm)
        dc_acc[g] = mm(jnp.concatenate([dm_hi, dm_lo], axis=1), jnp.concatenate([b, b], axis=0))
        db_acc[g] = mm(jnp.concatenate([dm_hi, dm_lo], axis=0), jnp.concatenate([c, c], axis=0), 0, 0)

    loop(0, GROUPS // 2, local)

    def y_copy(t):
        return remote(yout.at[t], yin.at[t], y_sem, (t,), (t,), {"tensor": me - row * 2 * CHIPS})

    def ret_copy(j, t):
        return remote(
            rout.at[j, t], rin.at[x, t], ret_sem, (j, t), (x, t), {"tensor": row * 2 * CHIPS + 2 * j + core}
        )

    def ret_arrival(q, t):
        return remote(rout.at[q, t], rin.at[q, t], ret_sem, (q, t), (q, t), {"tensor": sib})

    def hand_back(j, t):
        @pl.when(j != x)
        def _():
            ret_copy(j, t).start()

        @pl.when(j == x)
        def _():
            rin[x, t] = rout[j, t]

    def factor(j, t):
        return cin[j, t, SUB : SUB + HEADS_SUB, :]

    for t in range(SUBS):
        for j in range(CHIPS):

            @pl.when(j != x)
            def _():
                in_arrival(j, t).wait_recv()

        state = cin[CHIPS - 1, t, 0:SUB, :]
        for j in range(CHIPS - 2, -1, -1):
            rout[j, t] = state
            state = cin[j, t, 0:SUB, :] + expand(factor(j, t)) * state
        yout[t] = state

        @pl.when(row == 1)
        def _():
            y_copy(t).start()
            for j in range(CHIPS - 1):
                hand_back(j, t)

    @pl.when(last_pair)
    def _():
        rin[...] = jnp.zeros(rin.shape, F32)

    loop(GROUPS // 2, GROUPS, local)

    def made_copy(g):
        return remote(mout.at[g], est.at[g], made_sem, (g,), (g,), {"tensor": sib})

    def even_states(g):
        @pl.when(pair > 0)
        def _():
            for i in range(2):
                t = 2 * g + i

                @pl.when(t != me)
                def _():
                    saved_arrival(t).wait_recv()

                est[g, i] = esaved[t].astype(F32)

        @pl.when(pair == 0)
        def _():
            est[g] = jnp.zeros(est.shape[1:], F32)

        hi, lo = split2(xt[g].astype(F32) * expand(w_s[g]))
        m = bm[g]
        added = mm(jnp.concatenate([hi, lo], axis=1), jnp.concatenate([m, m], axis=0))
        mout[g] = (expand(f_s[g]) * est[g].reshape(ROWS, N) + added).reshape(mout.shape[1:])
        made_copy(g).start()

    @pl.when(even)
    def _():
        loop(0, GROUPS, even_states)

    @pl.when(row == 0)
    def _():
        for t in range(SUBS):
            y_copy(t).wait_recv()
            coming = yin[t]
            rout[CHIPS - 1, t] = coming
            through = factor(CHIPS - 1, t)
            for j in range(CHIPS - 2, -1, -1):
                rout[j, t] = rout[j, t] + expand(through) * coming
                through = through * factor(j, t)
            for j in range(CHIPS):
                hand_back(j, t)

    def from_states(g):
        @pl.when(core == 1)
        def _():
            made_copy(g).wait_recv()

        e_state = est[g].reshape(ROWS, N)
        e_hi, e_lo = split2(e_state)
        c = cm[g]
        ey = expand(e_s[g]) * yt[g].astype(F32)
        ey_hi, ey_lo = split2(ey)
        ec = mm(jnp.concatenate([e_hi, e_lo], axis=1), jnp.concatenate([c, c], axis=1), 1, 1)
        r_s[g] = r_s[g] + head_sums(ey * ec)
        dc_acc[g] = dc_acc[g] + mm(ey_hi, e_hi, 0, 0) + mm(ey_hi, e_lo, 0, 0) + mm(ey_lo, e_hi, 0, 0)

    loop(0, GROUPS, from_states)

    def g_copy(q, t):
        g = 2 * q + core
        return remote(gout.at[q, t], gst.at[g, t], g_sem, (q, t), (q, t), {"tensor": sib})

    def own_gradient(q):
        g = 2 * q + core
        f_odd = jnp.where(even, fsib[g], f_s[g])
        for t in range(SUBS):

            @pl.when(jnp.logical_and(q != x, jnp.logical_not(last_pair)))
            def _():
                ret_arrival(q, t).wait_recv()

            coming = rin[q, t]
            d_odd = jnp.where(even, dsib[q, t], d_s[g, t])
            to_even = d_odd + expand(f_odd[t * HEADS_SUB : (t + 1) * HEADS_SUB]) * coming
            gst[g, t] = jnp.where(even, to_even, coming)
            gout[q, t] = jnp.where(even, coming, to_even)
            g_copy(q, t).start()

    loop(0, CHIPS, own_gradient)

    lane = lax.broadcasted_iota(jnp.int32, (PER, Q), 1)

    def from_gradient(g):
        b = bm[g]
        g_state = gst[g].reshape(ROWS, N)
        g_hi, g_lo = split2(g_state)
        gb = mm(jnp.concatenate([g_hi, g_lo], axis=1), jnp.concatenate([b, b], axis=1), 1, 1)
        xf, yf = xt[g].astype(F32), yt[g].astype(F32)
        ex_w = expand(w_s[g])
        wx = ex_w * xf
        wx_hi, wx_lo = split2(wx)
        ends = head_sums(wx * gb)
        db_acc[g] = db_acc[g] + mm(wx_hi, g_hi, 0, 0) + mm(wx_hi, g_lo, 0, 0) + mm(wx_lo, g_hi, 0, 0)
        dx = dxt[g] + ex_w * gb + expand(skip_s[g]) * yf
        dx_ref[:, spans(g, ROWS)] = dx.T.astype(BF16)
        a, sg = a_s[g], s_s[g]
        e_state = est[g].reshape(ROWS, N)
        through = jnp.sum(head_sums(e_state * g_state), axis=1, keepdims=True) * f_s[g]
        at_end = through + jnp.sum(ends, axis=1, keepdims=True)
        u = u_s[g]
        dcum = r_s[g] - u - ends + jnp.where(lane == Q - 1, at_end, 0.0)
        drate = lane_sums(dcum, (iota(0) >= iota(1)).astype(F32).astype(BF16))
        drate_s[g] = (-a * drate + (u + ends) / sg) * sig_s[g]
        decay_part = jnp.sum(drate * (-a * sg), axis=1, keepdims=True)
        skip_part = jnp.sum(head_sums(yf * xf), axis=1, keepdims=True)
        z_s[g] = jnp.where(lane < Q // 2, decay_part, skip_part)

    loop(0, CHIPS, lambda q: from_gradient(2 * q + core))

    def sibs_gradient(q):
        for t in range(SUBS):
            g_copy(q, t).wait_recv()
        from_gradient(2 * q + 1 - core)

    loop(0, CHIPS, sibs_gradient)

    def exchange(n, dev, at, source, landing, base, beside):
        def copy(j):
            return remote(source(j), landing.at[at], sum_sem, (base + j,), (base + j,), dev(j))

        loop(1, n, lambda j: copy(j).start())
        landing[at] = source(0)[...]
        beside()
        loop(1, n, lambda j: copy(j).wait())
        return jnp.sum(landing[...], axis=0)

    def z_part(j):
        t = lax.rem(me + j, n_t)
        return z_s.at[t // 2, spans(lax.rem(t, 2), 8), :]

    def write_maps(acc, out):
        for g in range(GROUPS):
            wide_f32[pl.ds(g, Q, stride=GROUPS), :] = acc[g]
        out[...] = wide_f32[...].astype(BF16)

    def write_step():
        draw_ref[...] = drate_s[...].reshape(HEADS, Q).T

    part[0] = exchange(n_t, dev_t, me, z_part, from_t, 0, lambda: write_maps(db_acc, db_ref))
    part[1] = exchange(n_i, dev_i, inner, lambda j: part.at[0], from_i, n_t, lambda: write_maps(dc_acc, dc_ref))
    total_ref[...] = exchange(n_o, dev_o, outer, lambda j: part.at[1], from_o, n_t + n_i, write_step)

    def sent_saved(k):
        @pl.when(me != 2 * k)
        def _():
            saved_copy(k).wait_send()

    loop(1, n_t // 2, sent_saved)

    def sent(q):
        d_copy(q).wait_send()
        for t in range(SUBS):
            g_copy(q, t).wait_send()

            @pl.when(q != x)
            def _():
                in_copy(q, t).wait_send()

                @pl.when(jnp.logical_or(row == 0, q < CHIPS - 1))
                def _():
                    ret_copy(q, t).wait_send()

    loop(0, CHIPS, sent)

    @pl.when(row == 1)
    def _():
        for t in range(SUBS):
            y_copy(t).wait_send()

    @pl.when(even)
    def _():
        loop(0, GROUPS, lambda g: made_copy(g).wait_send())


def on_device(features, step_raw, input_map, output_map, decay_log, skip_gain, saved_states, grad_out):
    n_t = lax.axis_size("tensor")
    n_dp = lax.axis_size("dp")
    own = jnp.broadcast_to(jnp.concatenate([decay_log, skip_gain])[:, None], (16, Q))
    whole = pl.BlockSpec(memory_space=VMEM)
    dp_inner = 8 if n_dp % 8 == 0 else n_dp
    dp_outer = n_dp // dp_inner
    sums = n_t + dp_inner + dp_outer
    table = VMEM((GROUPS, PER, Q), F32)
    turned = VMEM((GROUPS, ROWS, Q), BF16)
    states = VMEM((GROUPS, SUBS, SUB, N), F32)
    quarters = VMEM((CHIPS, SUBS, SUB, N), F32)
    wires = VMEM((CHIPS, SUBS, WIRE, N), F32)
    eighth = VMEM((SUBS, SUB, N), F32)
    chunk = HEADS * PW // n_t
    halves = VMEM((GROUPS, 2, chunk, N), F32)
    maps = VMEM((GROUPS, Q, N), F32)
    sems = pltpu.SemaphoreType.DMA
    dx, draw, db, dc, total = pl.pallas_call(
        functools.partial(kernel, dp_inner),
        out_shape=[
            jax.ShapeDtypeStruct((Q, HEADS * PW), BF16),
            jax.ShapeDtypeStruct((Q, HEADS), F32),
            jax.ShapeDtypeStruct((Q * GROUPS, N), BF16),
            jax.ShapeDtypeStruct((Q * GROUPS, N), BF16),
            jax.ShapeDtypeStruct((8, Q), F32),
        ],
        in_specs=[whole] * 7,
        out_specs=[whole] * 5,
        scratch_shapes=[
            VMEM((n_t, 16, Q), F32), *([table] * 14),
            VMEM((GROUPS, Q, N), BF16), VMEM((GROUPS, Q, N), BF16), VMEM((Q * GROUPS, N), F32),
            turned, turned, states, quarters, wires, wires, quarters, eighth, eighth, quarters, states, quarters,
            VMEM((n_t, chunk, N), BF16), halves, halves, VMEM((GROUPS, ROWS, Q), F32), maps, maps,
            VMEM((2, 8, Q), F32),
            VMEM((n_t, 8, Q), F32), VMEM((dp_inner, 8, Q), F32), VMEM((dp_outer, 8, Q), F32),
            sems((2, n_t)), sems((2, n_t)), sems((2, 1)), sems((2, CHIPS)), sems((2, CHIPS, SUBS)), sems((2, SUBS)),
            sems((2, CHIPS, SUBS)), sems((2, CHIPS, SUBS)), sems((2, GROUPS)), sems((2, sums)),
        ],
        compiler_params=pltpu.CompilerParams(vmem_limit_bytes=LIMIT, collective_id=0, has_side_effects=True),
        name="scan_backward",
    )(
        step_raw, own, features, grad_out, input_map.reshape(Q * GROUPS, N), output_map.reshape(Q * GROUPS, N),
        saved_states.reshape(-1, chunk, N),
    )
    return (
        dx,
        draw,
        db.reshape(Q, GROUPS, N),
        dc.reshape(Q, GROUPS, N),
        total[:, 0],
        total[:, Q // 2],
    )


def solution(mesh):
    placed = (
        P(("dp", "tensor"), None),
        P(("dp", "tensor"), None),
        P(("dp", "tensor"), None, None),
        P(("dp", "tensor"), None, None),
        P("tensor"),
        P("tensor"),
        P("dp", None, "tensor", None, None),
        P(("dp", "tensor"), None),
    )
    return jax.shard_map(
        on_device,
        mesh=mesh,
        in_specs=placed,
        out_specs=(
            P(("dp", "tensor"), None),
            P(("dp", "tensor"), None),
            P(("dp", "tensor"), None, None),
            P(("dp", "tensor"), None, None),
            P("tensor"),
            P("tensor"),
        ),
        check_vma=False,
    )
```

```python
import functools

import jax
import jax.numpy as jnp
from jax import lax
from jax.experimental import pallas as pl
from jax.experimental.pallas import tpu as pltpu
from jax.sharding import PartitionSpec as P

MESH = pl.DeviceIdType.MESH
F32 = jnp.float32
BF16 = jnp.bfloat16
VMEM = pltpu.VMEM
LIMIT = 56 * 1024 * 1024

Q = 128
N = 128
PW = 32
HEADS = 128
GROUPS = 8
PER = HEADS // GROUPS
ROWS = PER * PW


def split2(x):
    hi = x.astype(BF16)
    return hi, (x - hi.astype(F32)).astype(BF16)


def split3(x):
    hi = x.astype(BF16)
    rest = x - hi.astype(F32)
    mid = rest.astype(BF16)
    return hi, mid, (rest - mid.astype(F32)).astype(BF16)


def mm(a, b, ca=1, cb=0):
    return lax.dot_general(a, b, (((ca,), (cb,)), ((), ())), preferred_element_type=F32)


def lane_sums(x, ones):
    return mm(jnp.concatenate(split3(x), axis=1), jnp.concatenate([ones] * 3, axis=0))


def iota(dim):
    return lax.broadcasted_iota(jnp.int32, (Q, Q), dim)


def expand(x):
    return jnp.broadcast_to(x[:, None, :], (x.shape[0], PW, x.shape[1])).reshape(-1, x.shape[1])


def head_sums(x):
    return x.reshape(-1, PW, x.shape[1]).sum(axis=1)

CHIPS = 4
SUBS = 4
SUB = ROWS // SUBS
HEADS_SUB = PER // SUBS
WIRE = SUB + 8


def loop(lo, hi, body):
    def step(i, carry):
        body(i)
        return carry

    lax.fori_loop(lo, hi, step, 0)


def several(lo, hi, at_once, body):
    def step(k):
        for j in range(at_once):
            body(lo + at_once * k + j)

    loop(0, (hi - lo) // at_once, step)


def spans(i, size):
    return pl.ds(pl.multiple_of(i * size, size), size)


def kernel(
    dp_inner,
    dl_ref, sk_ref, raw_hbm, x_hbm, y_hbm, b_hbm, c_hbm, saved_hbm,
    dx_hbm, draw_hbm, db_hbm, dc_hbm, total_ref,
    raw_s, x_s, y_s, b_in, c_in, saved_s, own_s,
    gath, fsib, e4, f4, w4, k4, ends4, thr4,
    cum_s, v_s, u_s, r_s, z_s, s_s, sig_s, a_s, fall_s, draw_s, wide_f32, bm, cm, xt, yt,
    d_own, d_out, dsib, comp, cin, rout, yout, yin, rin, g_own, g_out, g_sib,
    esaved, est, mout, dxt, gb_s, dx_s, db_acc, dc_acc,
    part, from_t, from_i, from_o,
    load_sem, own_sem, saved_sem, f_sem, d_sem, in_sem, y_sem, ret_sem, g_sem, made_sem, sum_sem, store_sem,
):
    me = lax.axis_index("tensor")
    rep = lax.axis_index("dp")
    n_t, n_i, n_o = from_t.shape[0], from_i.shape[0], from_o.shape[0]
    core = lax.rem(me, 2)
    even = core == 0
    pair = me // 2
    x = lax.rem(pair, CHIPS)
    row = pair // CHIPS
    sib = me + 1 - 2 * core
    inner, outer = lax.rem(rep, dp_inner), rep // dp_inner
    last_pair = pair == n_t // 2 - 1

    def dev_t(j):
        return {"tensor": lax.rem(me + j, n_t)}

    def dev_i(j):
        return {"dp": outer * dp_inner + lax.rem(inner + j, n_i)}

    def dev_o(j):
        return {"dp": lax.rem(outer + j, n_o) * dp_inner + inner}

    def remote(src, dst, sems, i, j, dev):
        return pltpu.make_async_remote_copy(
            src_ref=src, dst_ref=dst, send_sem=sems.at[(0, *i)], recv_sem=sems.at[(1, *j)],
            device_id=dev, device_id_type=MESH,
        )

    loads = [
        pltpu.make_async_copy(src, dst, load_sem.at[i])
        for i, (src, dst) in enumerate(
            ((raw_hbm, raw_s), (saved_hbm, saved_s), (b_hbm, b_in), (c_hbm, c_in), (y_hbm, y_s), (x_hbm, x_s))
        )
    ]
    for load in loads:
        load.start()
    barrier = pltpu.get_barrier_semaphore()
    for n, dev in ((n_t, dev_t), (n_i, dev_i), (n_o, dev_o)):
        loop(1, n, lambda j: pl.semaphore_signal(barrier, inc=1, device_id=dev(j), device_id_type=MESH))
    for h in range(8):
        own_s[h : h + 1, :] = jnp.full((1, Q), dl_ref[h], F32)
        own_s[8 + h : 9 + h, :] = jnp.full((1, Q), sk_ref[h], F32)
    loads[0].wait()
    raw = raw_s[...].astype(F32).T
    small = jnp.exp(-jnp.abs(raw))
    s = jnp.maximum(raw, 0.0) + jnp.log1p(small)
    sig_s[...] = jnp.where(raw >= 0, 1.0, small) / (1.0 + small)
    s_s[...] = s
    loads[1].wait()
    pl.semaphore_wait(barrier, n_t - 1 + n_i - 1 + n_o - 1)

    def own_copy(j):
        return remote(own_s, gath.at[me], own_sem, (j,), (j,), dev_t(j))

    def saved_copy(k):
        return remote(saved_s.at[k - 1], esaved.at[me], saved_sem, (k,), (me,), {"tensor": 2 * k})

    def saved_arrival(t):
        return remote(saved_s.at[0], esaved.at[t], saved_sem, (0,), (t,), {"tensor": sib})

    def send_saved(k):
        @pl.when(me != 2 * k)
        def _():
            saved_copy(k).start()

        @pl.when(me == 2 * k)
        def _():
            esaved[me] = saved_s[k - 1]

    loop(1, n_t, lambda j: own_copy(j).start())
    loop(1, n_t // 2, send_saved)
    gath[me] = own_s[...]

    loads[2].wait()
    loads[3].wait()
    for src, dst in ((b_in, bm), (c_in, cm)):
        wide_f32[...] = src[...].astype(F32)
        for g in range(GROUPS):
            dst[g] = wide_f32[pl.ds(g, Q, stride=GROUPS), :].astype(BF16)
    loads[4].wait()
    loads[5].wait()

    def turn(g):
        for src, dst in ((y_s, yt), (x_s, xt)):
            dst[g] = src[:, spans(g, ROWS)].astype(F32).T.astype(BF16)

    loop(0, GROUPS, turn)

    loop(1, n_t, lambda j: own_copy(j).wait())
    a = jnp.exp(gath[:, 0:8, :].reshape(HEADS, Q))
    a_s[...] = a
    k4[...] = gath[:, 8:16, :].reshape(k4.shape)
    cum = lane_sums(-a * s, (iota(0) <= iota(1)).astype(F32).astype(BF16))
    last = jnp.broadcast_to(cum[:, Q - 1 : Q], (HEADS, Q))
    fall = jnp.exp(last)
    fall_s[...] = fall
    f4[...] = fall.reshape(f4.shape)
    f_copy = remote(f4, fsib, f_sem, (0,), (0,), {"tensor": sib})
    f_copy.start()
    e4[...] = jnp.exp(cum).reshape(e4.shape)

    def sub_rows(t):
        return spans(t, SUB)

    def d_copy(t):
        return remote(d_out.at[t], dsib.at[t], d_sem, (t,), (t,), {"tensor": sib})

    def d_of(g, t):
        hi, lo = split2(yt[g, sub_rows(t), :].astype(F32) * expand(e4[g, t]))
        m = cm[g]
        return mm(jnp.concatenate([hi, lo], axis=1), jnp.concatenate([m, m], axis=0))

    def made(t):
        for q in range(CHIPS):
            d_out[t, q] = d_of(2 * q + 1 - core, t)
        d_copy(t).start()
        for q in range(CHIPS):
            d_own[t, q] = d_of(2 * q + core, t)

    def in_copy(t, q):
        return remote(
            comp.at[t, q], cin.at[t, x], in_sem, (t, q), (t, x), {"tensor": row * 2 * CHIPS + 2 * q + core}
        )

    def in_arrival(t, j):
        return remote(comp.at[t, j], cin.at[t, j], in_sem, (t, j), (t, j), {"tensor": sib})

    def fold(t):
        d_copy(t).wait_recv()

        def quarter(q):
            g = 2 * q + core
            f_here, f_there = f4[g, t], fsib[g, t]
            f_even, f_odd = jnp.where(even, f_here, f_there), jnp.where(even, f_there, f_here)
            d_here, d_there = d_own[t, q], dsib[t, q]
            d_even, d_odd = jnp.where(even, d_here, d_there), jnp.where(even, d_there, d_here)
            comp[t, q, 0:SUB, :] = d_even + expand(f_even) * d_odd
            f_both = f_even * f_odd
            comp[t, q, SUB:WIRE, :] = jnp.concatenate([f_both, f_both], axis=0)

            @pl.when(q != x)
            def _():
                in_copy(t, q).start()

            @pl.when(q == x)
            def _():
                cin[t, x] = comp[t, q]

        loop(0, CHIPS, quarter)

    made(0)
    made(1)
    f_copy.wait()
    fold(0)
    made(2)
    fold(1)
    made(3)
    fold(2)
    fold(3)

    cum_s[...] = cum.reshape(cum_s.shape)
    v_s[...] = (cum - jnp.log(s_s[...])).reshape(v_s.shape)
    w4[...] = (jnp.exp(last - cum) * s_s[...]).reshape(w4.shape)

    @pl.when(last_pair)
    def _():
        rin[...] = jnp.zeros(rin.shape, F32)

    inside = iota(0) >= iota(1)
    head_of = iota(0) // PW
    lane = lax.broadcasted_iota(jnp.int32, (PER, Q), 1)

    def local(g):
        b, c = bm[g], cm[g]
        m = mm(c, b, 1, 1)
        v = v_s[g]
        cum_n = cum_s[g].T
        dm = jnp.zeros((Q, Q), F32)
        for q in range(PER // 4):
            x4 = xt[g, q * Q : (q + 1) * Q, :].astype(F32)
            wide = jnp.concatenate([jnp.where(head_of == h, x4, 0.0).astype(BF16) for h in range(4)], axis=1)
            y4 = y_s[:, pl.ds(pl.multiple_of(g * ROWS + q * Q, Q), Q)]
            ds4 = mm(y4, wide)
            for h in range(4):
                hh = 4 * q + h
                mine = slice(hh * PW, (hh + 1) * PW)
                xh, yh = xt[g, mine, :], yt[g, mine, :]
                spread = cum_n[:, hh : hh + 1] - v[hh : hh + 1, :]
                decay = jnp.exp(jnp.where(inside, spread, -1e30))
                scores = m * decay
                dm = dm + ds4[:, h * Q : (h + 1) * Q] * decay
                both = jnp.concatenate(split2(scores), axis=0)
                dxw = mm(jnp.concatenate([yh, yh], axis=1), both)
                within = mm(xh, both, 1, 1)
                within = within[:, :Q] + within[:, Q:]
                dxt[g, mine, :] = dxw
                u_s[g, hh : hh + 1, :] = jnp.sum(xh.astype(F32) * dxw, axis=0, keepdims=True)
                r_s[g, hh : hh + 1, :] = jnp.sum(yh.astype(F32) * within, axis=0, keepdims=True)
        dm_hi, dm_lo = split2(dm)
        dc_acc[g] = mm(jnp.concatenate([dm_hi, dm_lo], axis=1), jnp.concatenate([b, b], axis=0))
        db_acc[g] = mm(jnp.concatenate([dm_hi, dm_lo], axis=0), jnp.concatenate([c, c], axis=0), 0, 0)
        z_s[g] = jnp.broadcast_to(
            jnp.sum(head_sums(yt[g].astype(F32) * xt[g].astype(F32)), axis=1, keepdims=True), (PER, Q)
        )

    def y_copy(t):
        return remote(yout.at[t], yin.at[t], y_sem, (t,), (t,), {"tensor": me - row * 2 * CHIPS})

    def ret_copy(t, j):
        return remote(
            rout.at[t, j], rin.at[t, x], ret_sem, (t, j), (t, x), {"tensor": row * 2 * CHIPS + 2 * j + core}
        )

    def ret_arrival(t, q):
        return remote(rout.at[t, q], rin.at[t, q], ret_sem, (t, q), (t, q), {"tensor": sib})

    def hand_back(t, j):
        @pl.when(j != x)
        def _():
            ret_copy(t, j).start()

        @pl.when(j == x)
        def _():
            rin[t, x] = rout[t, j]

    def factor(t, j):
        return cin[t, j, SUB : SUB + HEADS_SUB, :]

    def scan(t):
        for j in range(CHIPS):

            @pl.when(j != x)
            def _():
                in_arrival(t, j).wait_recv()

        state = cin[t, CHIPS - 1, 0:SUB, :]
        for j in range(CHIPS - 2, -1, -1):
            rout[t, j] = state
            state = cin[t, j, 0:SUB, :] + expand(factor(t, j)) * state

        @pl.when(row == 1)
        def _():
            yout[t] = state
            y_copy(t).start()
            loop(0, CHIPS - 1, lambda j: hand_back(t, j))

    def row_back(t):
        @pl.when(row == 0)
        def _():
            y_copy(t).wait_recv()
            coming = yin[t]
            rout[t, CHIPS - 1] = coming
            through = factor(t, CHIPS - 1)
            for j in range(CHIPS - 2, -1, -1):
                rout[t, j] = rout[t, j] + expand(through) * coming
                if j > 0:
                    through = through * factor(t, j)
            loop(0, CHIPS, lambda j: hand_back(t, j))

    def made_copy(g):
        return remote(mout.at[g], est.at[g], made_sem, (g,), (g,), {"tensor": sib})

    def whole_group(x4):
        return jnp.concatenate([expand(x4[t]) for t in range(SUBS)], axis=0)

    def even_states(g):
        @pl.when(even)
        def _():
            @pl.when(pair > 0)
            def _():
                for i in range(2):
                    t = 2 * g + i

                    @pl.when(t != me)
                    def _():
                        saved_arrival(t).wait_recv()

                    est[g, i] = esaved[t].astype(F32)

            @pl.when(pair == 0)
            def _():
                est[g] = jnp.zeros(est.shape[1:], F32)

            hi, lo = split2(xt[g].astype(F32) * whole_group(w4[g]))
            m = bm[g]
            added = mm(jnp.concatenate([hi, lo], axis=1), jnp.concatenate([m, m], axis=0))
            mout[g] = (whole_group(f4[g]) * est[g].reshape(ROWS, N) + added).reshape(mout.shape[1:])
            made_copy(g).start()

    def arrived_states(g):
        @pl.when(core == 1)
        def _():
            made_copy(g).wait_recv()

    def from_states(g):
        e_state = est[g].reshape(ROWS, N)
        e_hi, e_lo = split2(e_state)
        c = cm[g]
        ey = whole_group(e4[g]) * yt[g].astype(F32)
        ey_hi, ey_lo = split2(ey)
        ec = mm(jnp.concatenate([e_hi, e_lo], axis=1), jnp.concatenate([c, c], axis=1), 1, 1)
        r_s[g] = r_s[g] + head_sums(ey * ec)
        dc_acc[g] = dc_acc[g] + mm(ey_hi, e_hi, 0, 0) + mm(ey_hi, e_lo, 0, 0) + mm(ey_lo, e_hi, 0, 0)

    def g_copy(t):
        return remote(g_out.at[t], g_sib.at[t], g_sem, (t,), (t,), {"tensor": sib})

    def coming_back(t):
        def quarter(q):
            g = 2 * q + core

            @pl.when(jnp.logical_and(q != x, jnp.logical_not(last_pair)))
            def _():
                ret_arrival(t, q).wait_recv()

            coming = rin[t, q]
            f_odd = jnp.where(even, fsib[g, t], f4[g, t])
            d_odd = jnp.where(even, dsib[t, q], d_own[t, q])
            to_even = d_odd + expand(f_odd) * coming
            g_own[t, q] = jnp.where(even, to_even, coming)
            g_out[t, q] = jnp.where(even, coming, to_even)

        loop(0, CHIPS, quarter)
        g_copy(t).start()

    def step_part(g, t, state):
        b = bm[g]
        gb = mm(jnp.concatenate(split2(state), axis=1), jnp.concatenate([b, b], axis=1), 1, 1)
        gb_s[g, sub_rows(t), :] = gb
        wx = expand(w4[g, t]) * xt[g, sub_rows(t), :].astype(F32)
        ends4[g, t] = head_sums(wx * gb)
        e_state = est[g, t // 2, spans(t % 2, SUB), :]
        thr4[g, t] = jnp.broadcast_to(
            jnp.sum(head_sums(e_state * state), axis=1, keepdims=True), (HEADS_SUB, Q)
        )

    def map_part(g, t, state):
        xf, yf = xt[g, sub_rows(t), :].astype(F32), yt[g, sub_rows(t), :].astype(F32)
        ex_w = expand(w4[g, t])
        g_hi, g_lo = split2(state)
        wx_hi, wx_lo = split2(ex_w * xf)
        db_acc[g] = db_acc[g] + mm(wx_hi, g_hi, 0, 0) + mm(wx_hi, g_lo, 0, 0) + mm(wx_lo, g_hi, 0, 0)
        dx = dxt[g, sub_rows(t), :] + ex_w * gb_s[g, sub_rows(t), :] + expand(k4[g, t]) * yf
        dx_s[:, pl.ds(pl.multiple_of(g * ROWS + t * SUB, SUB), SUB)] = dx.T.astype(BF16)

    def steps(t):
        for q in range(CHIPS):
            step_part(2 * q + core, t, g_own[t, q])
        g_copy(t).wait_recv()
        for q in range(CHIPS):
            step_part(2 * q + 1 - core, t, g_sib[t, q])

    def maps(t):
        def quarter(q):
            map_part(2 * q + core, t, g_own[t, q])
            map_part(2 * q + 1 - core, t, g_sib[t, q])

        several(0, CHIPS, 2, quarter)

    loop(0, 3, local)
    scan(0)
    loop(3, 5, local)
    scan(1)
    loop(5, 7, local)
    scan(2)
    loop(7, 8, local)
    loop(0, 4, even_states)
    scan(3)
    loop(4, 8, even_states)
    row_back(0)
    loop(0, 4, arrived_states)
    several(0, 4, 2, from_states)
    row_back(1)
    loop(4, 8, arrived_states)
    several(4, 8, 2, from_states)
    coming_back(0)
    row_back(2)
    steps(0)
    coming_back(1)
    row_back(3)
    maps(0)
    coming_back(2)
    steps(1)
    maps(1)
    coming_back(3)
    steps(2)
    maps(2)
    steps(3)

    lanes = lax.broadcasted_iota(jnp.int32, (HEADS, Q), 1)
    ends = ends4[...].reshape(HEADS, Q)
    u = u_s[...].reshape(HEADS, Q)
    at_end = thr4[...].reshape(HEADS, Q) * fall_s[...] + jnp.sum(ends, axis=1, keepdims=True)
    dcum = r_s[...].reshape(HEADS, Q) - u - ends + jnp.where(lanes == Q - 1, at_end, 0.0)
    drate = lane_sums(dcum, (iota(0) >= iota(1)).astype(F32).astype(BF16))
    ra = a_s[...]
    rs = s_s[...]
    decay_part = jnp.sum(drate * (-ra * rs), axis=1, keepdims=True)
    z_s[...] = jnp.where(lanes < Q // 2, decay_part, z_s[...].reshape(HEADS, Q)).reshape(z_s.shape)

    def exchange(n, dev, at, source, landing, base, beside):
        def copy(j):
            return remote(source(j), landing.at[at], sum_sem, (base + j,), (base + j,), dev(j))

        loop(1, n, lambda j: copy(j).start())
        landing[at] = source(0)[...]
        beside()
        loop(1, n, lambda j: copy(j).wait())
        return jnp.sum(landing[...], axis=0)

    def z_part(j):
        t = lax.rem(me + j, n_t)
        return z_s.at[t // 2, spans(lax.rem(t, 2), 8), :]

    stores = [
        pltpu.make_async_copy(src, dst, store_sem.at[i])
        for i, (src, dst) in enumerate(((dx_s, dx_hbm), (draw_s, draw_hbm), (b_in, db_hbm), (c_in, dc_hbm)))
    ]

    def write_maps(acc, out):
        for g in range(GROUPS):
            wide_f32[pl.ds(g, Q, stride=GROUPS), :] = acc[g]
        out[...] = wide_f32[...].astype(BF16)

    def beside_t():
        maps(3)
        stores[0].start()

    def beside_i():
        draw_s[...] = ((-ra * drate + (u + ends) / rs) * sig_s[...]).T
        stores[1].start()
        write_maps(db_acc, b_in)
        stores[2].start()

    def beside_o():
        write_maps(dc_acc, c_in)
        stores[3].start()

    part[0] = exchange(n_t, dev_t, me, z_part, from_t, 0, beside_t)
    part[1] = exchange(n_i, dev_i, inner, lambda j: part.at[0], from_i, n_t, beside_i)
    total_ref[...] = exchange(n_o, dev_o, outer, lambda j: part.at[1], from_o, n_t + n_i, beside_o)

    for store in stores:
        store.wait()

    def sent_saved(k):
        @pl.when(me != 2 * k)
        def _():
            saved_copy(k).wait_send()

    loop(1, n_t // 2, sent_saved)

    def sent(t):
        d_copy(t).wait_send()
        g_copy(t).wait_send()

        @pl.when(row == 1)
        def _():
            y_copy(t).wait_send()

        def quarter(q):
            @pl.when(q != x)
            def _():
                in_copy(t, q).wait_send()

                @pl.when(jnp.logical_or(row == 0, q < CHIPS - 1))
                def _():
                    ret_copy(t, q).wait_send()

        loop(0, CHIPS, quarter)

    loop(0, SUBS, sent)

    @pl.when(even)
    def _():
        loop(0, GROUPS, lambda g: made_copy(g).wait_send())


def finish_kernel(dx_in, draw_in, db_in, dc_in, total_ref, dx, draw, db, dc, decay, skip):
    for src, dst in ((dx_in, dx), (draw_in, draw), (db_in, db), (dc_in, dc)):
        dst[...] = src[...]
    turned = total_ref[...].T
    decay[...] = turned[0, :]
    skip[...] = turned[Q // 2, :]


def on_device(features, step_raw, input_map, output_map, decay_log, skip_gain, saved_states, grad_out):
    n_t = lax.axis_size("tensor")
    n_dp = lax.axis_size("dp")
    whole = pl.BlockSpec(memory_space=VMEM)
    away = pl.BlockSpec(memory_space=pl.ANY)
    scalars = pl.BlockSpec(memory_space=pltpu.SMEM)
    dp_inner = 8 if n_dp % 8 == 0 else n_dp
    dp_outer = n_dp // dp_inner
    sums = n_t + dp_inner + dp_outer
    table = VMEM((HEADS, Q), F32)
    by_group = VMEM((GROUPS, PER, Q), F32)
    by_sub = VMEM((GROUPS, SUBS, HEADS_SUB, Q), F32)
    turned = VMEM((GROUPS, ROWS, Q), BF16)
    quarters = VMEM((SUBS, CHIPS, SUB, N), F32)
    wires = VMEM((SUBS, CHIPS, WIRE, N), F32)
    eighth = VMEM((SUBS, SUB, N), F32)
    chunk = HEADS * PW // n_t
    halves = VMEM((GROUPS, 2, chunk, N), F32)
    maps = VMEM((GROUPS, Q, N), F32)
    by_rows = VMEM((GROUPS, ROWS, Q), F32)
    flat_map = VMEM((Q * GROUPS, N), BF16)
    wide = VMEM((Q, HEADS * PW), BF16)
    sems = pltpu.SemaphoreType.DMA
    shapes = [
        jax.ShapeDtypeStruct((Q, HEADS * PW), BF16),
        jax.ShapeDtypeStruct((Q, HEADS), F32),
        jax.ShapeDtypeStruct((Q * GROUPS, N), BF16),
        jax.ShapeDtypeStruct((Q * GROUPS, N), BF16),
    ]
    results = pl.pallas_call(
        functools.partial(kernel, dp_inner),
        out_shape=[*shapes, jax.ShapeDtypeStruct((8, Q), F32)],
        in_specs=[scalars] * 2 + [away] * 6,
        out_specs=[away] * 4 + [whole],
        scratch_shapes=[
            VMEM((Q, HEADS), BF16), wide, wide, flat_map, flat_map, VMEM((n_t // 2 - 1, chunk, N), BF16),
            VMEM((16, Q), F32),
            VMEM((n_t, 16, Q), F32), *([by_sub] * 7),
            *([by_group] * 5), *([table] * 5),
            VMEM((Q * GROUPS, N), F32), VMEM((GROUPS, Q, N), BF16), VMEM((GROUPS, Q, N), BF16), turned, turned,
            *([quarters] * 3), wires, wires, quarters, eighth, eighth, *([quarters] * 4),
            VMEM((n_t, chunk, N), BF16), halves, halves, by_rows, by_rows, wide, maps, maps,
            VMEM((2, 8, Q), F32),
            VMEM((n_t, 8, Q), F32), VMEM((dp_inner, 8, Q), F32), VMEM((dp_outer, 8, Q), F32),
            sems((6,)), sems((2, n_t)), sems((2, n_t)), sems((2, 1)), sems((2, SUBS)), sems((2, SUBS, CHIPS)),
            sems((2, SUBS)), sems((2, SUBS, CHIPS)), sems((2, SUBS)), sems((2, GROUPS)), sems((2, sums)), sems((4,)),
        ],
        compiler_params=pltpu.CompilerParams(vmem_limit_bytes=LIMIT, collective_id=0, has_side_effects=True),
        name="scan_backward",
    )(
        decay_log, skip_gain, step_raw, features, grad_out, input_map.reshape(Q * GROUPS, N),
        output_map.reshape(Q * GROUPS, N), saved_states.reshape(-1, chunk, N),
    )
    vector = jax.ShapeDtypeStruct((8,), F32)
    dx, draw, db, dc, decay, skip = pl.pallas_call(
        finish_kernel,
        out_shape=[*shapes, vector, vector],
        in_specs=[whole] * 5,
        out_specs=[whole] * 6,
        compiler_params=pltpu.CompilerParams(vmem_limit_bytes=LIMIT),
        name="finish",
    )(*results)
    return (dx, draw, db.reshape(Q, GROUPS, N), dc.reshape(Q, GROUPS, N), decay, skip)


def solution(mesh):
    placed = (
        P(("dp", "tensor"), None),
        P(("dp", "tensor"), None),
        P(("dp", "tensor"), None, None),
        P(("dp", "tensor"), None, None),
        P("tensor"),
        P("tensor"),
        P("dp", None, "tensor", None, None),
        P(("dp", "tensor"), None),
    )
    return jax.shard_map(
        on_device,
        mesh=mesh,
        in_specs=placed,
        out_specs=(
            P(("dp", "tensor"), None),
            P(("dp", "tensor"), None),
            P(("dp", "tensor"), None, None),
            P(("dp", "tensor"), None, None),
            P("tensor"),
            P("tensor"),
        ),
        check_vma=False,
    )
```

```python
import functools

import jax
import jax.numpy as jnp
from jax import lax
from jax.experimental import pallas as pl
from jax.experimental.pallas import tpu as pltpu
from jax.sharding import PartitionSpec as P

MESH = pl.DeviceIdType.MESH
F32 = jnp.float32
BF16 = jnp.bfloat16
VMEM = pltpu.VMEM
LIMIT = 56 * 1024 * 1024

Q = 128
N = 128
PW = 32
HEADS = 128
GROUPS = 8
PER = HEADS // GROUPS
ROWS = PER * PW


def split2(x):
    hi = x.astype(BF16)
    return hi, (x - hi.astype(F32)).astype(BF16)


def split3(x):
    hi = x.astype(BF16)
    rest = x - hi.astype(F32)
    mid = rest.astype(BF16)
    return hi, mid, (rest - mid.astype(F32)).astype(BF16)


def mm(a, b, ca=1, cb=0):
    return lax.dot_general(a, b, (((ca,), (cb,)), ((), ())), preferred_element_type=F32)


def lane_sums(x, ones):
    return mm(jnp.concatenate(split3(x), axis=1), jnp.concatenate([ones] * 3, axis=0))


def iota(dim):
    return lax.broadcasted_iota(jnp.int32, (Q, Q), dim)


def expand(x):
    return jnp.broadcast_to(x[:, None, :], (x.shape[0], PW, x.shape[1])).reshape(-1, x.shape[1])


def head_sums(x):
    return x.reshape(-1, PW, x.shape[1]).sum(axis=1)

CHIPS = 4
SUBS = 4
SUB = ROWS // SUBS
HEADS_SUB = PER // SUBS
WIRE = SUB + 8


def loop(lo, hi, body):
    def step(i, carry):
        body(i)
        return carry

    lax.fori_loop(lo, hi, step, 0)


def several(lo, hi, at_once, body):
    def step(k):
        for j in range(at_once):
            body(lo + at_once * k + j)

    loop(0, (hi - lo) // at_once, step)


def spans(i, size):
    return pl.ds(pl.multiple_of(i * size, size), size)


def kernel(
    dp_inner,
    dl_ref, sk_ref, raw_hbm, x_hbm, y_hbm, b_hbm, c_hbm, saved_hbm,
    dx_hbm, draw_hbm, db_hbm, dc_hbm, total_ref,
    raw_s, x_s, y_s, b_in, c_in, saved_s, own_s,
    gath, fsib, e4, f4, w4, k4, ends4, thr4,
    cum_s, v_s, u_s, r_s, z_s, s_s, sig_s, a_s, fall_s, draw_s, wide_f32, bm, cm, xt, yt,
    d_own, d_out, dsib, comp, cin, rout, yout, yin, rin, g_own, g_out, g_sib,
    esaved, est, mout, dxt, gb_s, dx_s, db_acc, dc_acc,
    z_out, part_x, part_y, from_x, from_y, from_z,
    load_sem, own_sem, saved_sem, f_sem, d_sem, in_sem, y_sem, ret_sem, g_sem, made_sem, sum_sem, store_sem,
):
    me = lax.axis_index("tensor")
    rep = lax.axis_index("dp")
    n_t = gath.shape[0]
    n_x, n_y, n_z = from_x.shape[0], from_y.shape[0], from_z.shape[0]
    core = lax.rem(me, 2)
    even = core == 0
    pair = me // 2
    x = lax.rem(pair, CHIPS)
    row = pair // CHIPS
    sib = me + 1 - 2 * core
    place = lax.rem(me, n_x)
    z_at, y_low = lax.rem(rep, dp_inner), rep // dp_inner
    y_lows = n_y // (n_t // n_x)
    y_at = row * y_lows + y_low
    last_pair = pair == n_t // 2 - 1

    def dev_t(j):
        return {"tensor": lax.rem(me + j, n_t)}

    def dev_x(j):
        return {"tensor": row * n_x + lax.rem(place + j, n_x)}

    def y_of(j):
        return lax.rem(y_at + j, n_y)

    def dev_y(j):
        return {"tensor": y_of(j) // y_lows * n_x + place, "dp": lax.rem(y_of(j), y_lows) * dp_inner + z_at}

    def dev_z(j):
        return {"dp": y_low * dp_inner + lax.rem(z_at + j, n_z)}

    def remote(src, dst, sems, i, j, dev):
        return pltpu.make_async_remote_copy(
            src_ref=src, dst_ref=dst, send_sem=sems.at[(0, *i)], recv_sem=sems.at[(1, *j)],
            device_id=dev, device_id_type=MESH,
        )

    loads = [
        pltpu.make_async_copy(src, dst, load_sem.at[i])
        for i, (src, dst) in enumerate(
            ((raw_hbm, raw_s), (saved_hbm, saved_s), (b_hbm, b_in), (c_hbm, c_in), (y_hbm, y_s), (x_hbm, x_s))
        )
    ]
    for load in loads:
        load.start()
    barrier = pltpu.get_barrier_semaphore()

    def greet(dev):
        pl.semaphore_signal(barrier, inc=1, device_id=dev, device_id_type=MESH)

    def greet_y(j):
        @pl.when(lax.rem(y_of(j), y_lows) != y_low)
        def _():
            greet(dev_y(j))

    loop(1, n_t, lambda j: greet(dev_t(j)))
    loop(1, n_y, greet_y)
    loop(1, n_z, lambda j: greet(dev_z(j)))
    spot = lax.broadcasted_iota(jnp.int32, (1, Q), 1)
    params = jnp.zeros((1, Q), F32)
    for h in range(8):
        params = jnp.where(spot == h, dl_ref[h], params)
        params = jnp.where(spot == 8 + h, sk_ref[h], params)
    own_s[...] = params
    loads[0].wait()
    raw = raw_s[...].astype(F32).T
    small = jnp.exp(-jnp.abs(raw))
    s = jnp.maximum(raw, 0.0) + jnp.log1p(small)
    sig_s[...] = jnp.where(raw >= 0, 1.0, small) / (1.0 + small)
    s_s[...] = s
    loads[1].wait()
    pl.semaphore_wait(barrier, n_t - 1 + n_y - n_y // y_lows + n_z - 1)

    def own_copy(j):
        return remote(own_s, gath.at[me], own_sem, (j,), (j,), dev_t(lax.rem(j + 3, n_t - 1) + 1))

    def saved_copy(k):
        return remote(saved_s.at[k - 1], esaved.at[me], saved_sem, (k,), (me,), {"tensor": 2 * k})

    def saved_arrival(t):
        return remote(saved_s.at[0], esaved.at[t], saved_sem, (0,), (t,), {"tensor": sib})

    def send_saved(k):
        @pl.when(me != 2 * k)
        def _():
            saved_copy(k).start()

        @pl.when(me == 2 * k)
        def _():
            esaved[me] = saved_s[k - 1]

    loop(1, n_t, lambda j: own_copy(j).start())
    loop(1, n_t // 2, send_saved)
    gath[me] = own_s[...]

    loads[2].wait()
    loads[3].wait()
    for src, dst in ((b_in, bm), (c_in, cm)):
        wide_f32[...] = src[...].astype(F32)
        for g in range(GROUPS):
            dst[g] = wide_f32[pl.ds(g, Q, stride=GROUPS), :].astype(BF16)
    loads[4].wait()
    loads[5].wait()

    def turn(g):
        for src, dst in ((y_s, yt), (x_s, xt)):
            dst[g] = src[:, spans(g, ROWS)].astype(F32).T.astype(BF16)

    loop(0, GROUPS, turn)

    loop(1, n_t, lambda j: own_copy(j).wait())
    params = gath[...].reshape(n_t, Q)
    for h in range(8):
        a_s[pl.ds(h, n_t, stride=8), :] = jnp.broadcast_to(params[:, h : h + 1], (n_t, Q))
        draw_s[pl.ds(h, n_t, stride=8), :] = jnp.broadcast_to(params[:, 8 + h : 9 + h], (n_t, Q))
    a = jnp.exp(a_s[...])
    a_s[...] = a
    k4[...] = draw_s[...].reshape(k4.shape)
    cum = lane_sums(-a * s, (iota(0) <= iota(1)).astype(F32).astype(BF16))
    last = jnp.broadcast_to(cum[:, Q - 1 : Q], (HEADS, Q))
    fall = jnp.exp(last)
    fall_s[...] = fall
    f4[...] = fall.reshape(f4.shape)
    f_copy = remote(f4, fsib, f_sem, (0,), (0,), {"tensor": sib})
    f_copy.start()
    e4[...] = jnp.exp(cum).reshape(e4.shape)

    def sub_rows(t):
        return spans(t, SUB)

    def d_copy(t):
        return remote(d_out.at[t], dsib.at[t], d_sem, (t,), (t,), {"tensor": sib})

    def d_of(g, t):
        hi, lo = split2(yt[g, sub_rows(t), :].astype(F32) * expand(e4[g, t]))
        m = cm[g]
        return mm(jnp.concatenate([hi, lo], axis=1), jnp.concatenate([m, m], axis=0))

    def made(t):
        for q in range(CHIPS):
            d_out[t, q] = d_of(2 * q + 1 - core, t)
        d_copy(t).start()
        for q in range(CHIPS):
            d_own[t, q] = d_of(2 * q + core, t)

    def in_copy(t, q):
        return remote(
            comp.at[t, q], cin.at[t, x], in_sem, (t, q), (t, x), {"tensor": row * 2 * CHIPS + 2 * q + core}
        )

    def in_arrival(t, j):
        return remote(comp.at[t, j], cin.at[t, j], in_sem, (t, j), (t, j), {"tensor": sib})

    def fold(t):
        d_copy(t).wait_recv()

        def quarter(q):
            g = 2 * q + core
            f_here, f_there = f4[g, t], fsib[g, t]
            f_even, f_odd = jnp.where(even, f_here, f_there), jnp.where(even, f_there, f_here)
            d_here, d_there = d_own[t, q], dsib[t, q]
            d_even, d_odd = jnp.where(even, d_here, d_there), jnp.where(even, d_there, d_here)
            comp[t, q, 0:SUB, :] = d_even + expand(f_even) * d_odd
            f_both = f_even * f_odd
            comp[t, q, SUB:WIRE, :] = jnp.concatenate([f_both, f_both], axis=0)

            @pl.when(q != x)
            def _():
                in_copy(t, q).start()

            @pl.when(q == x)
            def _():
                cin[t, x] = comp[t, q]

        loop(0, CHIPS, quarter)

    made(0)
    made(1)
    f_copy.wait()
    fold(0)
    made(2)
    fold(1)
    made(3)
    fold(2)
    fold(3)

    cum_s[...] = cum.reshape(cum_s.shape)
    v_s[...] = (cum - jnp.log(s_s[...])).reshape(v_s.shape)
    w4[...] = (jnp.exp(last - cum) * s_s[...]).reshape(w4.shape)

    @pl.when(last_pair)
    def _():
        rin[...] = jnp.zeros(rin.shape, F32)

    inside = iota(0) >= iota(1)
    head_of = iota(0) // PW
    lane = lax.broadcasted_iota(jnp.int32, (PER, Q), 1)

    def local(g):
        b, c = bm[g], cm[g]
        m = mm(c, b, 1, 1)
        v = v_s[g]
        cum_n = cum_s[g].T
        dm = jnp.zeros((Q, Q), F32)
        for q in range(PER // 4):
            x4 = xt[g, q * Q : (q + 1) * Q, :].astype(F32)
            wide = jnp.concatenate([jnp.where(head_of == h, x4, 0.0).astype(BF16) for h in range(4)], axis=1)
            y4 = y_s[:, pl.ds(pl.multiple_of(g * ROWS + q * Q, Q), Q)]
            ds4 = mm(y4, wide)
            for h in range(4):
                hh = 4 * q + h
                mine = slice(hh * PW, (hh + 1) * PW)
                xh, yh = xt[g, mine, :], yt[g, mine, :]
                spread = cum_n[:, hh : hh + 1] - v[hh : hh + 1, :]
                decay = jnp.exp(jnp.where(inside, spread, -1e30))
                scores = m * decay
                dm = dm + ds4[:, h * Q : (h + 1) * Q] * decay
                both = jnp.concatenate(split2(scores), axis=0)
                dxw = mm(jnp.concatenate([yh, yh], axis=1), both)
                within = mm(xh, both, 1, 1)
                within = within[:, :Q] + within[:, Q:]
                dxt[g, mine, :] = dxw
                u_s[g, hh : hh + 1, :] = jnp.sum(xh.astype(F32) * dxw, axis=0, keepdims=True)
                r_s[g, hh : hh + 1, :] = jnp.sum(yh.astype(F32) * within, axis=0, keepdims=True)
        dm_hi, dm_lo = split2(dm)
        dc_acc[g] = mm(jnp.concatenate([dm_hi, dm_lo], axis=1), jnp.concatenate([b, b], axis=0))
        db_acc[g] = mm(jnp.concatenate([dm_hi, dm_lo], axis=0), jnp.concatenate([c, c], axis=0), 0, 0)
        z_s[g] = jnp.broadcast_to(
            jnp.sum(head_sums(yt[g].astype(F32) * xt[g].astype(F32)), axis=1, keepdims=True), (PER, Q)
        )

    def y_copy(t):
        return remote(yout.at[t], yin.at[t], y_sem, (t,), (t,), {"tensor": me - row * 2 * CHIPS})

    def ret_copy(t, j):
        return remote(
            rout.at[t, j], rin.at[t, x], ret_sem, (t, j), (t, x), {"tensor": row * 2 * CHIPS + 2 * j + core}
        )

    def ret_arrival(t, q):
        return remote(rout.at[t, q], rin.at[t, q], ret_sem, (t, q), (t, q), {"tensor": sib})

    def hand_back(t, j):
        @pl.when(j != x)
        def _():
            ret_copy(t, j).start()

        @pl.when(j == x)
        def _():
            rin[t, x] = rout[t, j]

    def factor(t, j):
        return cin[t, j, SUB : SUB + HEADS_SUB, :]

    def scan(t):
        for j in range(CHIPS):

            @pl.when(j != x)
            def _():
                in_arrival(t, j).wait_recv()

        state = cin[t, CHIPS - 1, 0:SUB, :]
        for j in range(CHIPS - 2, -1, -1):
            rout[t, j] = state
            state = cin[t, j, 0:SUB, :] + expand(factor(t, j)) * state

        @pl.when(row == 1)
        def _():
            yout[t] = state
            y_copy(t).start()
            loop(0, CHIPS - 1, lambda j: hand_back(t, j))

    def row_back(t):
        @pl.when(row == 0)
        def _():
            y_copy(t).wait_recv()
            coming = yin[t]
            rout[t, CHIPS - 1] = coming
            through = factor(t, CHIPS - 1)
            for j in range(CHIPS - 2, -1, -1):
                rout[t, j] = rout[t, j] + expand(through) * coming
                if j > 0:
                    through = through * factor(t, j)
            loop(0, CHIPS, lambda j: hand_back(t, j))

    def made_copy(g):
        return remote(mout.at[g], est.at[g], made_sem, (g,), (g,), {"tensor": sib})

    def whole_group(x4):
        return jnp.concatenate([expand(x4[t]) for t in range(SUBS)], axis=0)

    def even_states(g):
        @pl.when(even)
        def _():
            @pl.when(pair > 0)
            def _():
                for i in range(2):
                    t = 2 * g + i

                    @pl.when(t != me)
                    def _():
                        saved_arrival(t).wait_recv()

                    est[g, i] = esaved[t].astype(F32)

            @pl.when(pair == 0)
            def _():
                est[g] = jnp.zeros(est.shape[1:], F32)

            hi, lo = split2(xt[g].astype(F32) * whole_group(w4[g]))
            m = bm[g]
            added = mm(jnp.concatenate([hi, lo], axis=1), jnp.concatenate([m, m], axis=0))
            mout[g] = (whole_group(f4[g]) * est[g].reshape(ROWS, N) + added).reshape(mout.shape[1:])
            made_copy(g).start()

    def arrived_states(g):
        @pl.when(core == 1)
        def _():
            made_copy(g).wait_recv()

    def from_states(g):
        e_state = est[g].reshape(ROWS, N)
        e_hi, e_lo = split2(e_state)
        c = cm[g]
        ey = whole_group(e4[g]) * yt[g].astype(F32)
        ey_hi, ey_lo = split2(ey)
        ec = mm(jnp.concatenate([e_hi, e_lo], axis=1), jnp.concatenate([c, c], axis=1), 1, 1)
        r_s[g] = r_s[g] + head_sums(ey * ec)
        dc_acc[g] = dc_acc[g] + mm(ey_hi, e_hi, 0, 0) + mm(ey_hi, e_lo, 0, 0) + mm(ey_lo, e_hi, 0, 0)

    def g_copy(t):
        return remote(g_out.at[t], g_sib.at[t], g_sem, (t,), (t,), {"tensor": sib})

    def coming_back(t):
        def quarter(q):
            g = 2 * q + core

            @pl.when(jnp.logical_and(q != x, jnp.logical_not(last_pair)))
            def _():
                ret_arrival(t, q).wait_recv()

            coming = rin[t, q]
            f_odd = jnp.where(even, fsib[g, t], f4[g, t])
            d_odd = jnp.where(even, dsib[t, q], d_own[t, q])
            to_even = d_odd + expand(f_odd) * coming
            g_own[t, q] = jnp.where(even, to_even, coming)
            g_out[t, q] = jnp.where(even, coming, to_even)

        loop(0, CHIPS, quarter)
        g_copy(t).start()

    def step_part(g, t, state):
        b = bm[g]
        gb = mm(jnp.concatenate(split2(state), axis=1), jnp.concatenate([b, b], axis=1), 1, 1)
        gb_s[g, sub_rows(t), :] = gb
        wx = expand(w4[g, t]) * xt[g, sub_rows(t), :].astype(F32)
        ends4[g, t] = head_sums(wx * gb)
        e_state = est[g, t // 2, spans(t % 2, SUB), :]
        thr4[g, t] = jnp.broadcast_to(
            jnp.sum(head_sums(e_state * state), axis=1, keepdims=True), (HEADS_SUB, Q)
        )

    def map_part(g, t, state):
        xf, yf = xt[g, sub_rows(t), :].astype(F32), yt[g, sub_rows(t), :].astype(F32)
        ex_w = expand(w4[g, t])
        g_hi, g_lo = split2(state)
        wx_hi, wx_lo = split2(ex_w * xf)
        db_acc[g] = db_acc[g] + mm(wx_hi, g_hi, 0, 0) + mm(wx_hi, g_lo, 0, 0) + mm(wx_lo, g_hi, 0, 0)
        dx = dxt[g, sub_rows(t), :] + ex_w * gb_s[g, sub_rows(t), :] + expand(k4[g, t]) * yf
        dx_s[:, pl.ds(pl.multiple_of(g * ROWS + t * SUB, SUB), SUB)] = dx.T.astype(BF16)

    def steps(t):
        for q in range(CHIPS):
            step_part(2 * q + core, t, g_own[t, q])
        g_copy(t).wait_recv()
        for q in range(CHIPS):
            step_part(2 * q + 1 - core, t, g_sib[t, q])

    def maps(t):
        def quarter(q):
            map_part(2 * q + core, t, g_own[t, q])
            map_part(2 * q + 1 - core, t, g_sib[t, q])

        several(0, CHIPS, 2, quarter)

    loop(0, 3, local)
    scan(0)
    loop(3, 5, local)
    scan(1)
    loop(5, 7, local)
    scan(2)
    loop(7, 8, local)
    scan(3)
    row_back(0)
    row_back(1)
    loop(0, GROUPS, even_states)
    row_back(2)
    row_back(3)
    coming_back(0)
    loop(0, GROUPS, arrived_states)
    several(0, GROUPS, 2, from_states)
    coming_back(1)
    steps(0)
    maps(0)
    coming_back(2)
    steps(1)
    maps(1)
    coming_back(3)
    steps(2)
    maps(2)
    steps(3)

    lanes = lax.broadcasted_iota(jnp.int32, (HEADS, Q), 1)
    ends = ends4[...].reshape(HEADS, Q)
    u = u_s[...].reshape(HEADS, Q)
    at_end = thr4[...].reshape(HEADS, Q) * fall_s[...] + jnp.sum(ends, axis=1, keepdims=True)
    dcum = r_s[...].reshape(HEADS, Q) - u - ends + jnp.where(lanes == Q - 1, at_end, 0.0)
    drate = lane_sums(dcum, (iota(0) >= iota(1)).astype(F32).astype(BF16))
    ra = a_s[...]
    rs = s_s[...]
    decay_part = jnp.sum(drate * (-ra * rs), axis=1, keepdims=True)
    turned = jnp.where(lanes < Q // 2, decay_part, z_s[...].reshape(HEADS, Q)).T
    z_out[...] = jnp.concatenate([turned[0:1], turned[Q // 2 : Q // 2 + 1]], axis=0)

    def exchange(n, dev, at, source, landing, base, beside):
        def copy(j):
            return remote(source, landing.at[at], sum_sem, (base + j,), (base + j,), dev(j))

        loop(1, n, lambda j: copy(j).start())
        landing[at] = source[...]
        beside()
        loop(1, n, lambda j: copy(j).wait())
        return jnp.sum(landing[...], axis=0)

    stores = [
        pltpu.make_async_copy(src, dst, store_sem.at[i])
        for i, (src, dst) in enumerate(((dx_s, dx_hbm), (draw_s, draw_hbm), (b_in, db_hbm), (c_in, dc_hbm)))
    ]

    def write_maps(acc, out):
        for g in range(GROUPS):
            wide_f32[pl.ds(g, Q, stride=GROUPS), :] = acc[g]
        out[...] = wide_f32[...].astype(BF16)

    def beside_x():
        maps(3)
        stores[0].start()

    def beside_y():
        draw_s[...] = ((-ra * drate + (u + ends) / rs) * sig_s[...]).T
        stores[1].start()
        write_maps(db_acc, b_in)
        stores[2].start()

    def beside_z():
        write_maps(dc_acc, c_in)
        stores[3].start()

    part_x[...] = exchange(n_x, dev_x, place, z_out, from_x, 0, beside_x)
    part_y[...] = exchange(n_y, dev_y, y_at, part_x, from_y, n_x, beside_y)
    total = exchange(n_z, dev_z, z_at, part_y, from_z, n_x + n_y, beside_z)
    mine = (iota(0) == 8 * me + iota(1)).astype(F32).astype(BF16)
    total_ref[...] = lane_sums(jnp.concatenate([total] * 4, axis=0), mine)

    for store in stores:
        store.wait()

    def sent_saved(k):
        @pl.when(me != 2 * k)
        def _():
            saved_copy(k).wait_send()

    loop(1, n_t // 2, sent_saved)

    def sent(t):
        d_copy(t).wait_send()
        g_copy(t).wait_send()

        @pl.when(row == 1)
        def _():
            y_copy(t).wait_send()

        def quarter(q):
            @pl.when(q != x)
            def _():
                in_copy(t, q).wait_send()

                @pl.when(jnp.logical_or(row == 0, q < CHIPS - 1))
                def _():
                    ret_copy(t, q).wait_send()

        loop(0, CHIPS, quarter)

    loop(0, SUBS, sent)

    @pl.when(even)
    def _():
        loop(0, GROUPS, lambda g: made_copy(g).wait_send())


def finish_kernel(dx_in, draw_in, db_in, dc_in, total_ref, dx, draw, db, dc, decay, skip):
    for src, dst in ((dx_in, dx), (draw_in, draw), (db_in, db), (dc_in, dc)):
        dst[...] = src[...]
    decay[...] = total_ref[0, 0:8]
    skip[...] = total_ref[1, 0:8]


def on_device(features, step_raw, input_map, output_map, decay_log, skip_gain, saved_states, grad_out):
    n_t = lax.axis_size("tensor")
    n_dp = lax.axis_size("dp")
    whole = pl.BlockSpec(memory_space=VMEM)
    away = pl.BlockSpec(memory_space=pl.ANY)
    scalars = pl.BlockSpec(memory_space=pltpu.SMEM)
    n_x = 2 * CHIPS
    n_z = 8 if n_dp % 8 == 0 else 1
    n_y = n_dp // n_z * (n_t // n_x)
    sums = n_x + n_y + n_z
    table = VMEM((HEADS, Q), F32)
    by_group = VMEM((GROUPS, PER, Q), F32)
    by_sub = VMEM((GROUPS, SUBS, HEADS_SUB, Q), F32)
    turned = VMEM((GROUPS, ROWS, Q), BF16)
    quarters = VMEM((SUBS, CHIPS, SUB, N), F32)
    wires = VMEM((SUBS, CHIPS, WIRE, N), F32)
    eighth = VMEM((SUBS, SUB, N), F32)
    chunk = HEADS * PW // n_t
    halves = VMEM((GROUPS, 2, chunk, N), F32)
    maps = VMEM((GROUPS, Q, N), F32)
    by_rows = VMEM((GROUPS, ROWS, Q), F32)
    flat_map = VMEM((Q * GROUPS, N), BF16)
    wide = VMEM((Q, HEADS * PW), BF16)
    sems = pltpu.SemaphoreType.DMA
    shapes = [
        jax.ShapeDtypeStruct((Q, HEADS * PW), BF16),
        jax.ShapeDtypeStruct((Q, HEADS), F32),
        jax.ShapeDtypeStruct((Q * GROUPS, N), BF16),
        jax.ShapeDtypeStruct((Q * GROUPS, N), BF16),
    ]
    results = pl.pallas_call(
        functools.partial(kernel, n_z),
        out_shape=[*shapes, jax.ShapeDtypeStruct((8, Q), F32)],
        in_specs=[scalars] * 2 + [away] * 6,
        out_specs=[away] * 4 + [whole],
        scratch_shapes=[
            VMEM((Q, HEADS), BF16), wide, wide, flat_map, flat_map, VMEM((n_t // 2 - 1, chunk, N), BF16),
            VMEM((1, Q), F32),
            VMEM((n_t, 1, Q), F32), *([by_sub] * 7),
            *([by_group] * 5), *([table] * 5),
            VMEM((Q * GROUPS, N), F32), VMEM((GROUPS, Q, N), BF16), VMEM((GROUPS, Q, N), BF16), turned, turned,
            *([quarters] * 3), wires, wires, quarters, eighth, eighth, *([quarters] * 4),
            VMEM((n_t, chunk, N), BF16), halves, halves, by_rows, by_rows, wide, maps, maps,
            VMEM((2, Q), F32), VMEM((2, Q), F32), VMEM((2, Q), F32),
            VMEM((n_x, 2, Q), F32), VMEM((n_y, 2, Q), F32), VMEM((n_z, 2, Q), F32),
            sems((6,)), sems((2, n_t)), sems((2, n_t)), sems((2, 1)), sems((2, SUBS)), sems((2, SUBS, CHIPS)),
            sems((2, SUBS)), sems((2, SUBS, CHIPS)), sems((2, SUBS)), sems((2, GROUPS)), sems((2, sums)), sems((4,)),
        ],
        compiler_params=pltpu.CompilerParams(vmem_limit_bytes=LIMIT, collective_id=0, has_side_effects=True),
        name="scan_backward",
    )(
        decay_log, skip_gain, step_raw, features, grad_out, input_map.reshape(Q * GROUPS, N),
        output_map.reshape(Q * GROUPS, N), saved_states.reshape(-1, chunk, N),
    )
    vector = jax.ShapeDtypeStruct((8,), F32)
    halves_of = [pl.BlockSpec((shape.shape[0] // 2, shape.shape[1]), lambda i: (i, 0)) for shape in shapes]
    dx, draw, db, dc, decay, skip = pl.pallas_call(
        finish_kernel,
        out_shape=[*shapes, vector, vector],
        grid=(2,),
        in_specs=[*halves_of, pl.BlockSpec((8, Q), lambda i: (0, 0))],
        out_specs=[*halves_of, *([pl.BlockSpec((8,), lambda i: (0,))] * 2)],
        compiler_params=pltpu.CompilerParams(vmem_limit_bytes=LIMIT),
        name="finish",
    )(*results)
    return (dx, draw, db.reshape(Q, GROUPS, N), dc.reshape(Q, GROUPS, N), decay, skip)


def solution(mesh):
    placed = (
        P(("dp", "tensor"), None),
        P(("dp", "tensor"), None),
        P(("dp", "tensor"), None, None),
        P(("dp", "tensor"), None, None),
        P("tensor"),
        P("tensor"),
        P("dp", None, "tensor", None, None),
        P(("dp", "tensor"), None),
    )
    return jax.shard_map(
        on_device,
        mesh=mesh,
        in_specs=placed,
        out_specs=(
            P(("dp", "tensor"), None),
            P(("dp", "tensor"), None),
            P(("dp", "tensor"), None, None),
            P(("dp", "tensor"), None, None),
            P("tensor"),
            P("tensor"),
        ),
        check_vma=False,
    )
```

```python
import functools

import jax
import jax.numpy as jnp
from jax import lax
from jax.experimental import pallas as pl
from jax.experimental.pallas import tpu as pltpu
from jax.sharding import PartitionSpec as P

MESH = pl.DeviceIdType.MESH
F32 = jnp.float32
BF16 = jnp.bfloat16
VMEM = pltpu.VMEM
LIMIT = 56 * 1024 * 1024

Q = 128
N = 128
PW = 32
HEADS = 128
GROUPS = 8
PER = HEADS // GROUPS
ROWS = PER * PW


def split2(x):
    hi = x.astype(BF16)
    return hi, (x - hi.astype(F32)).astype(BF16)


def split3(x):
    hi = x.astype(BF16)
    rest = x - hi.astype(F32)
    mid = rest.astype(BF16)
    return hi, mid, (rest - mid.astype(F32)).astype(BF16)


def mm(a, b, ca=1, cb=0):
    return lax.dot_general(a, b, (((ca,), (cb,)), ((), ())), preferred_element_type=F32)


def lane_sums(x, ones):
    return mm(jnp.concatenate(split3(x), axis=1), jnp.concatenate([ones] * 3, axis=0))


def iota(dim):
    return lax.broadcasted_iota(jnp.int32, (Q, Q), dim)


def expand(x):
    return jnp.broadcast_to(x[:, None, :], (x.shape[0], PW, x.shape[1])).reshape(-1, x.shape[1])


def head_sums(x):
    return x.reshape(-1, PW, x.shape[1]).sum(axis=1)

CHIPS = 4
SUBS = 4
SUB = ROWS // SUBS
HEADS_SUB = PER // SUBS
WIRE = SUB + 8


def loop(lo, hi, body):
    def step(i, carry):
        body(i)
        return carry

    lax.fori_loop(lo, hi, step, 0)


def each(lo, hi, body):
    for i in range(lo, hi):
        body(i)


def several(lo, hi, at_once, body):
    def step(k):
        for j in range(at_once):
            body(lo + at_once * k + j)

    loop(0, (hi - lo) // at_once, step)


def spans(i, size):
    return pl.ds(pl.multiple_of(i * size, size), size)


def kernel(
    dp_inner,
    dl_ref, sk_ref, raw_hbm, x_hbm, y_hbm, b_hbm, c_hbm, saved_hbm,
    dx_hbm, draw_hbm, db_hbm, dc_hbm, total_ref,
    raw_s, x_s, y_s, b_in, c_in, saved_s, own_s,
    gath, fsib, e4, f4, w4, k4, ends4, thr4,
    cum_s, v_s, u_s, r_s, z_s, s_s, sig_s, a_s, fall_s, draw_s, wide_f32, bm, cm, xt, yt,
    d_own, d_out, dsib, comp, cin, rout, yout, yin, rin, g_own, g_out, g_sib,
    esaved, est, mout, dxt, gb_s, dx_s, db_acc, dc_acc,
    z_out, part_x, part_y, from_x, from_y, from_z,
    load_sem, own_sem, saved_sem, f_sem, d_sem, in_sem, y_sem, ret_sem, g_sem, made_sem, sum_sem, store_sem,
):
    me = lax.axis_index("tensor")
    rep = lax.axis_index("dp")
    n_t = gath.shape[0]
    n_x, n_y, n_z = from_x.shape[0], from_y.shape[0], from_z.shape[0]
    core = lax.rem(me, 2)
    even = core == 0
    pair = me // 2
    x = lax.rem(pair, CHIPS)
    row = pair // CHIPS
    sib = me + 1 - 2 * core
    place = lax.rem(me, n_x)
    z_at, y_low = lax.rem(rep, dp_inner), rep // dp_inner
    y_lows = n_y // (n_t // n_x)
    y_at = row * y_lows + y_low
    last_pair = pair == n_t // 2 - 1

    def dev_t(j):
        return {"tensor": lax.rem(me + j, n_t)}

    def dev_x(j):
        return {"tensor": row * n_x + lax.rem(place + j, n_x)}

    def y_of(j):
        return lax.rem(y_at + j, n_y)

    def dev_y(j):
        return {"tensor": y_of(j) // y_lows * n_x + place, "dp": lax.rem(y_of(j), y_lows) * dp_inner + z_at}

    def dev_z(j):
        return {"dp": y_low * dp_inner + lax.rem(z_at + j, n_z)}

    def remote(src, dst, sems, i, j, dev):
        return pltpu.make_async_remote_copy(
            src_ref=src, dst_ref=dst, send_sem=sems.at[(0, *i)], recv_sem=sems.at[(1, *j)],
            device_id=dev, device_id_type=MESH,
        )

    loads = [
        pltpu.make_async_copy(src, dst, load_sem.at[i])
        for i, (src, dst) in enumerate(
            ((raw_hbm, raw_s), (saved_hbm, saved_s), (b_hbm, b_in), (c_hbm, c_in), (y_hbm, y_s), (x_hbm, x_s))
        )
    ]
    for load in loads:
        load.start()
    barrier = pltpu.get_barrier_semaphore()

    def greet(dev):
        pl.semaphore_signal(barrier, inc=1, device_id=dev, device_id_type=MESH)

    def greet_y(j):
        @pl.when(lax.rem(y_of(j), y_lows) != y_low)
        def _():
            greet(dev_y(j))

    each(1, n_t, lambda j: greet(dev_t(j)))
    each(1, n_y, greet_y)
    each(1, n_z, lambda j: greet(dev_z(j)))
    spot = lax.broadcasted_iota(jnp.int32, (1, Q), 1)
    params = jnp.zeros((1, Q), F32)
    for h in range(8):
        params = jnp.where(spot == h, dl_ref[h], params)
        params = jnp.where(spot == 8 + h, sk_ref[h], params)
    own_s[...] = params
    loads[0].wait()
    raw = raw_s[...].astype(F32).T
    small = jnp.exp(-jnp.abs(raw))
    s = jnp.maximum(raw, 0.0) + jnp.log1p(small)
    sig_s[...] = jnp.where(raw >= 0, 1.0, small) / (1.0 + small)
    s_s[...] = s
    loads[1].wait()
    pl.semaphore_wait(barrier, n_t - 1 + n_y - n_y // y_lows + n_z - 1)

    def own_copy(j):
        return remote(own_s, gath.at[me], own_sem, (j,), (j,), dev_t((j + 3) % (n_t - 1) + 1))

    def saved_copy(k):
        return remote(saved_s.at[k - 1], esaved.at[me], saved_sem, (k,), (me,), {"tensor": 2 * k})

    def saved_arrival(t):
        return remote(saved_s.at[0], esaved.at[t], saved_sem, (0,), (t,), {"tensor": sib})

    def send_saved(k):
        @pl.when(me != 2 * k)
        def _():
            saved_copy(k).start()

        @pl.when(me == 2 * k)
        def _():
            esaved[me] = saved_s[k - 1]

    each(1, n_t, lambda j: own_copy(j).start())
    loop(1, n_t // 2, send_saved)
    gath[me] = own_s[...]

    loads[2].wait()
    loads[3].wait()
    for src, dst in ((b_in, bm), (c_in, cm)):
        wide_f32[...] = src[...].astype(F32)
        for g in range(GROUPS):
            dst[g] = wide_f32[pl.ds(g, Q, stride=GROUPS), :].astype(BF16)
    loads[4].wait()
    loads[5].wait()

    def turn(g):
        for src, dst in ((y_s, yt), (x_s, xt)):
            dst[g] = src[:, spans(g, ROWS)].astype(F32).T.astype(BF16)

    loop(0, GROUPS, turn)

    each(1, n_t, lambda j: own_copy(j).wait())
    params = gath[...].reshape(n_t, Q)
    for h in range(8):
        a_s[pl.ds(h, n_t, stride=8), :] = jnp.broadcast_to(params[:, h : h + 1], (n_t, Q))
        draw_s[pl.ds(h, n_t, stride=8), :] = jnp.broadcast_to(params[:, 8 + h : 9 + h], (n_t, Q))
    a = jnp.exp(a_s[...])
    a_s[...] = a
    k4[...] = draw_s[...].reshape(k4.shape)
    cum = lane_sums(-a * s, (iota(0) <= iota(1)).astype(F32).astype(BF16))
    last = jnp.broadcast_to(cum[:, Q - 1 : Q], (HEADS, Q))
    fall = jnp.exp(last)
    fall_s[...] = fall
    f4[...] = fall.reshape(f4.shape)
    f_copy = remote(f4, fsib, f_sem, (0,), (0,), {"tensor": sib})
    f_copy.start()
    e4[...] = jnp.exp(cum).reshape(e4.shape)

    def sub_rows(t):
        return spans(t, SUB)

    def d_copy(t):
        return remote(d_out.at[t], dsib.at[t], d_sem, (t,), (t,), {"tensor": sib})

    def d_of(g, t):
        hi, lo = split2(yt[g, sub_rows(t), :].astype(F32) * expand(e4[g, t]))
        m = cm[g]
        return mm(jnp.concatenate([hi, lo], axis=1), jnp.concatenate([m, m], axis=0))

    def made(t):
        for q in range(CHIPS):
            d_out[t, q] = d_of(2 * q + 1 - core, t)
        d_copy(t).start()
        for q in range(CHIPS):
            d_own[t, q] = d_of(2 * q + core, t)

    def in_copy(t, q):
        return remote(
            comp.at[t, q], cin.at[t, x], in_sem, (t, q), (t, x), {"tensor": row * 2 * CHIPS + 2 * q + core}
        )

    def in_arrival(t, j):
        return remote(comp.at[t, j], cin.at[t, j], in_sem, (t, j), (t, j), {"tensor": sib})

    def fold(t):
        d_copy(t).wait_recv()

        def quarter(q):
            g = 2 * q + core
            f_here, f_there = f4[g, t], fsib[g, t]
            f_even, f_odd = jnp.where(even, f_here, f_there), jnp.where(even, f_there, f_here)
            d_here, d_there = d_own[t, q], dsib[t, q]
            d_even, d_odd = jnp.where(even, d_here, d_there), jnp.where(even, d_there, d_here)
            comp[t, q, 0:SUB, :] = d_even + expand(f_even) * d_odd
            f_both = f_even * f_odd
            comp[t, q, SUB:WIRE, :] = jnp.concatenate([f_both, f_both], axis=0)

            @pl.when(q != x)
            def _():
                in_copy(t, q).start()

            @pl.when(q == x)
            def _():
                cin[t, x] = comp[t, q]

        loop(0, CHIPS, quarter)

    made(0)
    made(1)
    f_copy.wait()
    fold(0)
    made(2)
    fold(1)
    made(3)
    fold(2)
    fold(3)

    cum_s[...] = cum.reshape(cum_s.shape)
    v_s[...] = (cum - jnp.log(s_s[...])).reshape(v_s.shape)
    w4[...] = (jnp.exp(last - cum) * s_s[...]).reshape(w4.shape)

    @pl.when(last_pair)
    def _():
        rin[...] = jnp.zeros(rin.shape, F32)

    inside = iota(0) >= iota(1)
    head_of = iota(0) // PW
    lane = lax.broadcasted_iota(jnp.int32, (PER, Q), 1)

    def local(g):
        b, c = bm[g], cm[g]
        m = mm(c, b, 1, 1)
        v = v_s[g]
        cum_n = cum_s[g].T
        dm = jnp.zeros((Q, Q), F32)
        for q in range(PER // 4):
            x4 = xt[g, q * Q : (q + 1) * Q, :].astype(F32)
            wide = jnp.concatenate([jnp.where(head_of == h, x4, 0.0).astype(BF16) for h in range(4)], axis=1)
            y4 = y_s[:, pl.ds(pl.multiple_of(g * ROWS + q * Q, Q), Q)]
            ds4 = mm(y4, wide)
            for h in range(4):
                hh = 4 * q + h
                mine = slice(hh * PW, (hh + 1) * PW)
                xh, yh = xt[g, mine, :], yt[g, mine, :]
                spread = cum_n[:, hh : hh + 1] - v[hh : hh + 1, :]
                decay = jnp.exp(jnp.where(inside, spread, -1e30))
                scores = m * decay
                dm = dm + ds4[:, h * Q : (h + 1) * Q] * decay
                both = jnp.concatenate(split2(scores), axis=0)
                dxw = mm(jnp.concatenate([yh, yh], axis=1), both)
                within = mm(xh, both, 1, 1)
                within = within[:, :Q] + within[:, Q:]
                dxt[g, mine, :] = dxw
                u_s[g, hh : hh + 1, :] = jnp.sum(xh.astype(F32) * dxw, axis=0, keepdims=True)
                r_s[g, hh : hh + 1, :] = jnp.sum(yh.astype(F32) * within, axis=0, keepdims=True)
        dm_hi, dm_lo = split2(dm)
        dc_acc[g] = mm(jnp.concatenate([dm_hi, dm_lo], axis=1), jnp.concatenate([b, b], axis=0))
        db_acc[g] = mm(jnp.concatenate([dm_hi, dm_lo], axis=0), jnp.concatenate([c, c], axis=0), 0, 0)
        z_s[g] = jnp.broadcast_to(
            jnp.sum(head_sums(yt[g].astype(F32) * xt[g].astype(F32)), axis=1, keepdims=True), (PER, Q)
        )

    def y_copy(t):
        return remote(yout.at[t], yin.at[t], y_sem, (t,), (t,), {"tensor": me - row * 2 * CHIPS})

    def ret_copy(t, j):
        return remote(
            rout.at[t, j], rin.at[t, x], ret_sem, (t, j), (t, x), {"tensor": row * 2 * CHIPS + 2 * j + core}
        )

    def ret_arrival(t, q):
        return remote(rout.at[t, q], rin.at[t, q], ret_sem, (t, q), (t, q), {"tensor": sib})

    def hand_back(t, j):
        @pl.when(j != x)
        def _():
            ret_copy(t, j).start()

        @pl.when(j == x)
        def _():
            rin[t, x] = rout[t, j]

    def factor(t, j):
        return cin[t, j, SUB : SUB + HEADS_SUB, :]

    def scan(t):
        for j in range(CHIPS):

            @pl.when(j != x)
            def _():
                in_arrival(t, j).wait_recv()

        state = cin[t, CHIPS - 1, 0:SUB, :]
        for j in range(CHIPS - 2, -1, -1):
            rout[t, j] = state
            state = cin[t, j, 0:SUB, :] + expand(factor(t, j)) * state

        @pl.when(row == 1)
        def _():
            yout[t] = state
            y_copy(t).start()
            loop(0, CHIPS - 1, lambda j: hand_back(t, j))

    def row_back(t):
        @pl.when(row == 0)
        def _():
            y_copy(t).wait_recv()
            coming = yin[t]
            rout[t, CHIPS - 1] = coming
            through = factor(t, CHIPS - 1)
            for j in range(CHIPS - 2, -1, -1):
                rout[t, j] = rout[t, j] + expand(through) * coming
                if j > 0:
                    through = through * factor(t, j)
            loop(0, CHIPS, lambda j: hand_back(t, j))

    def made_copy(g):
        return remote(mout.at[g], est.at[g], made_sem, (g,), (g,), {"tensor": sib})

    def whole_group(x4):
        return jnp.concatenate([expand(x4[t]) for t in range(SUBS)], axis=0)

    def even_states(g):
        @pl.when(even)
        def _():
            @pl.when(pair > 0)
            def _():
                for i in range(2):
                    t = 2 * g + i

                    @pl.when(t != me)
                    def _():
                        saved_arrival(t).wait_recv()

                    est[g, i] = esaved[t].astype(F32)

            @pl.when(pair == 0)
            def _():
                est[g] = jnp.zeros(est.shape[1:], F32)

            hi, lo = split2(xt[g].astype(F32) * whole_group(w4[g]))
            m = bm[g]
            added = mm(jnp.concatenate([hi, lo], axis=1), jnp.concatenate([m, m], axis=0))
            mout[g] = (whole_group(f4[g]) * est[g].reshape(ROWS, N) + added).reshape(mout.shape[1:])
            made_copy(g).start()

    def arrived_states(g):
        @pl.when(core == 1)
        def _():
            made_copy(g).wait_recv()

    def from_states(g):
        e_state = est[g].reshape(ROWS, N)
        e_hi, e_lo = split2(e_state)
        c = cm[g]
        ey = whole_group(e4[g]) * yt[g].astype(F32)
        ey_hi, ey_lo = split2(ey)
        ec = mm(jnp.concatenate([e_hi, e_lo], axis=1), jnp.concatenate([c, c], axis=1), 1, 1)
        r_s[g] = r_s[g] + head_sums(ey * ec)
        dc_acc[g] = dc_acc[g] + mm(ey_hi, e_hi, 0, 0) + mm(ey_hi, e_lo, 0, 0) + mm(ey_lo, e_hi, 0, 0)

    def g_copy(t):
        return remote(g_out.at[t], g_sib.at[t], g_sem, (t,), (t,), {"tensor": sib})

    def coming_back(t):
        def quarter(q):
            g = 2 * q + core

            @pl.when(jnp.logical_and(q != x, jnp.logical_not(last_pair)))
            def _():
                ret_arrival(t, q).wait_recv()

            coming = rin[t, q]
            f_odd = jnp.where(even, fsib[g, t], f4[g, t])
            d_odd = jnp.where(even, dsib[t, q], d_own[t, q])
            to_even = d_odd + expand(f_odd) * coming
            g_own[t, q] = jnp.where(even, to_even, coming)
            g_out[t, q] = jnp.where(even, coming, to_even)

        loop(0, CHIPS, quarter)
        g_copy(t).start()

    def step_part(g, t, state):
        b = bm[g]
        gb = mm(jnp.concatenate(split2(state), axis=1), jnp.concatenate([b, b], axis=1), 1, 1)
        gb_s[g, sub_rows(t), :] = gb
        wx = expand(w4[g, t]) * xt[g, sub_rows(t), :].astype(F32)
        ends4[g, t] = head_sums(wx * gb)
        e_state = est[g, t // 2, spans(t % 2, SUB), :]
        thr4[g, t] = jnp.broadcast_to(
            jnp.sum(head_sums(e_state * state), axis=1, keepdims=True), (HEADS_SUB, Q)
        )

    def map_part(g, t, state):
        xf, yf = xt[g, sub_rows(t), :].astype(F32), yt[g, sub_rows(t), :].astype(F32)
        ex_w = expand(w4[g, t])
        g_hi, g_lo = split2(state)
        wx_hi, wx_lo = split2(ex_w * xf)
        db_acc[g] = db_acc[g] + mm(wx_hi, g_hi, 0, 0) + mm(wx_hi, g_lo, 0, 0) + mm(wx_lo, g_hi, 0, 0)
        dx = dxt[g, sub_rows(t), :] + ex_w * gb_s[g, sub_rows(t), :] + expand(k4[g, t]) * yf
        dx_s[:, pl.ds(pl.multiple_of(g * ROWS + t * SUB, SUB), SUB)] = dx.T.astype(BF16)

    def steps(t):
        for q in range(CHIPS):
            step_part(2 * q + core, t, g_own[t, q])
        g_copy(t).wait_recv()
        for q in range(CHIPS):
            step_part(2 * q + 1 - core, t, g_sib[t, q])

    def maps(t):
        def quarter(q):
            map_part(2 * q + core, t, g_own[t, q])
            map_part(2 * q + 1 - core, t, g_sib[t, q])

        several(0, CHIPS, 2, quarter)

    loop(0, 3, local)
    scan(0)
    loop(3, 5, local)
    scan(1)
    loop(5, 7, local)
    scan(2)
    loop(7, 8, local)
    scan(3)
    row_back(0)
    row_back(1)
    loop(0, GROUPS, even_states)
    row_back(2)
    row_back(3)
    coming_back(0)
    loop(0, GROUPS, arrived_states)
    several(0, GROUPS, 2, from_states)
    coming_back(1)
    steps(0)
    maps(0)
    coming_back(2)
    steps(1)
    maps(1)
    coming_back(3)
    steps(2)
    maps(2)
    steps(3)

    lanes = lax.broadcasted_iota(jnp.int32, (HEADS, Q), 1)
    ends = ends4[...].reshape(HEADS, Q)
    u = u_s[...].reshape(HEADS, Q)
    at_end = thr4[...].reshape(HEADS, Q) * fall_s[...] + jnp.sum(ends, axis=1, keepdims=True)
    dcum = r_s[...].reshape(HEADS, Q) - u - ends + jnp.where(lanes == Q - 1, at_end, 0.0)
    drate = lane_sums(dcum, (iota(0) >= iota(1)).astype(F32).astype(BF16))
    ra = a_s[...]
    rs = s_s[...]
    decay_part = jnp.sum(drate * (-ra * rs), axis=1, keepdims=True)
    turned = jnp.where(lanes < Q // 2, decay_part, z_s[...].reshape(HEADS, Q)).T
    z_out[...] = jnp.concatenate([turned[0:1], turned[Q // 2 : Q // 2 + 1]], axis=0)

    def exchange(n, dev, at, source, landing, base, beside):
        def copy(j):
            return remote(source, landing.at[at], sum_sem, (base + j,), (base + j,), dev(j))

        each(1, n, lambda j: copy(j).start())
        landing[at] = source[...]
        beside()
        each(1, n, lambda j: copy(j).wait())
        return jnp.sum(landing[...], axis=0)

    stores = [
        pltpu.make_async_copy(src, dst, store_sem.at[i])
        for i, (src, dst) in enumerate(((dx_s, dx_hbm), (draw_s, draw_hbm), (b_in, db_hbm), (c_in, dc_hbm)))
    ]

    def write_maps(acc, out):
        for g in range(GROUPS):
            wide_f32[pl.ds(g, Q, stride=GROUPS), :] = acc[g]
        out[...] = wide_f32[...].astype(BF16)

    def beside_x():
        maps(3)
        stores[0].start()

    def beside_y():
        draw_s[...] = ((-ra * drate + (u + ends) / rs) * sig_s[...]).T
        stores[1].start()
        write_maps(db_acc, b_in)
        stores[2].start()

    def beside_z():
        write_maps(dc_acc, c_in)
        stores[3].start()

    part_x[...] = exchange(n_x, dev_x, place, z_out, from_x, 0, beside_x)
    part_y[...] = exchange(n_y, dev_y, y_at, part_x, from_y, n_x, beside_y)
    total = exchange(n_z, dev_z, z_at, part_y, from_z, n_x + n_y, beside_z)
    mine = (iota(0) == 8 * me + iota(1)).astype(F32).astype(BF16)
    total_ref[...] = lane_sums(jnp.concatenate([total] * 4, axis=0), mine)

    for store in stores:
        store.wait()

    def sent_saved(k):
        @pl.when(me != 2 * k)
        def _():
            saved_copy(k).wait_send()

    loop(1, n_t // 2, sent_saved)

    def sent(t):
        d_copy(t).wait_send()
        g_copy(t).wait_send()

        @pl.when(row == 1)
        def _():
            y_copy(t).wait_send()

        def quarter(q):
            @pl.when(q != x)
            def _():
                in_copy(t, q).wait_send()

                @pl.when(jnp.logical_or(row == 0, q < CHIPS - 1))
                def _():
                    ret_copy(t, q).wait_send()

        loop(0, CHIPS, quarter)

    loop(0, SUBS, sent)

    @pl.when(even)
    def _():
        loop(0, GROUPS, lambda g: made_copy(g).wait_send())


def finish_kernel(dx_in, draw_in, db_in, dc_in, total_ref, dx, draw, db, dc, decay, skip):
    for src, dst in ((dx_in, dx), (draw_in, draw), (db_in, db), (dc_in, dc)):
        dst[...] = src[...]
    decay[...] = total_ref[0, 0:8]
    skip[...] = total_ref[1, 0:8]


def on_device(features, step_raw, input_map, output_map, decay_log, skip_gain, saved_states, grad_out):
    n_t = lax.axis_size("tensor")
    n_dp = lax.axis_size("dp")
    whole = pl.BlockSpec(memory_space=VMEM)
    away = pl.BlockSpec(memory_space=pl.ANY)
    scalars = pl.BlockSpec(memory_space=pltpu.SMEM)
    n_x = 2 * CHIPS
    n_z = 8 if n_dp % 8 == 0 else 1
    n_y = n_dp // n_z * (n_t // n_x)
    sums = n_x + n_y + n_z
    table = VMEM((HEADS, Q), F32)
    by_group = VMEM((GROUPS, PER, Q), F32)
    by_sub = VMEM((GROUPS, SUBS, HEADS_SUB, Q), F32)
    turned = VMEM((GROUPS, ROWS, Q), BF16)
    quarters = VMEM((SUBS, CHIPS, SUB, N), F32)
    wires = VMEM((SUBS, CHIPS, WIRE, N), F32)
    eighth = VMEM((SUBS, SUB, N), F32)
    chunk = HEADS * PW // n_t
    halves = VMEM((GROUPS, 2, chunk, N), F32)
    maps = VMEM((GROUPS, Q, N), F32)
    by_rows = VMEM((GROUPS, ROWS, Q), F32)
    flat_map = VMEM((Q * GROUPS, N), BF16)
    wide = VMEM((Q, HEADS * PW), BF16)
    sems = pltpu.SemaphoreType.DMA
    shapes = [
        jax.ShapeDtypeStruct((Q, HEADS * PW), BF16),
        jax.ShapeDtypeStruct((Q, HEADS), F32),
        jax.ShapeDtypeStruct((Q * GROUPS, N), BF16),
        jax.ShapeDtypeStruct((Q * GROUPS, N), BF16),
    ]
    results = pl.pallas_call(
        functools.partial(kernel, n_z),
        out_shape=[*shapes, jax.ShapeDtypeStruct((8, Q), F32)],
        in_specs=[scalars] * 2 + [away] * 6,
        out_specs=[away] * 4 + [whole],
        scratch_shapes=[
            VMEM((Q, HEADS), BF16), wide, wide, flat_map, flat_map, VMEM((n_t // 2 - 1, chunk, N), BF16),
            VMEM((1, Q), F32),
            VMEM((n_t, 1, Q), F32), *([by_sub] * 7),
            *([by_group] * 5), *([table] * 5),
            VMEM((Q * GROUPS, N), F32), VMEM((GROUPS, Q, N), BF16), VMEM((GROUPS, Q, N), BF16), turned, turned,
            *([quarters] * 3), wires, wires, quarters, eighth, eighth, *([quarters] * 4),
            VMEM((n_t, chunk, N), BF16), halves, halves, by_rows, by_rows, wide, maps, maps,
            VMEM((2, Q), F32), VMEM((2, Q), F32), VMEM((2, Q), F32),
            VMEM((n_x, 2, Q), F32), VMEM((n_y, 2, Q), F32), VMEM((n_z, 2, Q), F32),
            sems((6,)), sems((2, n_t)), sems((2, n_t)), sems((2, 1)), sems((2, SUBS)), sems((2, SUBS, CHIPS)),
            sems((2, SUBS)), sems((2, SUBS, CHIPS)), sems((2, SUBS)), sems((2, GROUPS)), sems((2, sums)), sems((4,)),
        ],
        compiler_params=pltpu.CompilerParams(vmem_limit_bytes=LIMIT, collective_id=0, has_side_effects=True),
        name="scan_backward",
    )(
        decay_log, skip_gain, step_raw, features, grad_out, input_map.reshape(Q * GROUPS, N),
        output_map.reshape(Q * GROUPS, N), saved_states.reshape(-1, chunk, N),
    )
    vector = jax.ShapeDtypeStruct((8,), F32)
    halves_of = [pl.BlockSpec((shape.shape[0] // 2, shape.shape[1]), lambda i: (i, 0)) for shape in shapes]
    dx, draw, db, dc, decay, skip = pl.pallas_call(
        finish_kernel,
        out_shape=[*shapes, vector, vector],
        grid=(2,),
        in_specs=[*halves_of, pl.BlockSpec((8, Q), lambda i: (0, 0))],
        out_specs=[*halves_of, *([pl.BlockSpec((8,), lambda i: (0,))] * 2)],
        compiler_params=pltpu.CompilerParams(vmem_limit_bytes=LIMIT),
        name="finish",
    )(*results)
    return (dx, draw, db.reshape(Q, GROUPS, N), dc.reshape(Q, GROUPS, N), decay, skip)


def solution(mesh):
    placed = (
        P(("dp", "tensor"), None),
        P(("dp", "tensor"), None),
        P(("dp", "tensor"), None, None),
        P(("dp", "tensor"), None, None),
        P("tensor"),
        P("tensor"),
        P("dp", None, "tensor", None, None),
        P(("dp", "tensor"), None),
    )
    return jax.shard_map(
        on_device,
        mesh=mesh,
        in_specs=placed,
        out_specs=(
            P(("dp", "tensor"), None),
            P(("dp", "tensor"), None),
            P(("dp", "tensor"), None, None),
            P(("dp", "tensor"), None, None),
            P("tensor"),
            P("tensor"),
        ),
        check_vma=False,
    )
```
